256 devices in a mesh: comp: 16 (over x_lo, z), shard: 16 (over y, x_hi, core).
Axes of the slice: x: 4 (x_hi: 2, x_lo: 2; x = x_hi * 2 + x_lo), y: 4, z: 8, core: 2. Of those that a mesh axis runs over, the one named last changes fastest.
Arguments:
- modal_coefs: float32 [16, 16, 512, 256], P('comp', 'shard'), may hold values from -6 to 6
- comp_levels: int32 [16, 3], replicated, may hold values from 2 to 5, as said below
- comp_coefs: int32 [16], replicated, may hold values from -2 to 2, as said below
- velocity: float32 [4], replicated, may hold values from 0.5 to 2
Outputs:
- combined: float32 [16, 16, 512, 256], P('comp', 'shard')
The draws below stay inside these ranges and needn't reach their ends.
Inputs may be any that keep to these rules, and one draw needn't show every extreme that they name: `comp_levels`: each row sums to 9. `comp_coefs`: never zero.
All inputs are finite; a program needn't handle non-finite values.
Results may differ from the reference program's by a relative error of at most 0.0003.
Values sent between devices are 32-bit elements; how exact they have to be, the bound alone decides.
A program may use at most 64 MiB of HBM per device.

```python
import math
import jax
import jax.numpy as jnp
import numpy as np
from jax import lax

COEF = 256
BASE = 2
RISE = 3
GRID = 512
CELLS0 = 16
COMPS = 16


def composition_table():
    extremes = [(RISE, 0, 0), (0, RISE, 0), (0, 0, RISE)]
    others = [(one, two, RISE - one - two) for one in range(RISE + 1) for two in range(RISE + 1 - one)]
    return np.array(extremes + [entry for entry in others if entry not in extremes], dtype=np.int32)


def draw_comp_levels(key, part):
    key = jax.random.fold_in(key, 11)
    table = jnp.asarray(composition_table())
    choose_key, spot_key, pick_key = jax.random.split(key, 3)
    index = jax.random.randint(choose_key, (COMPS,), 0, table.shape[0])
    spot = jax.random.randint(spot_key, (), 0, COMPS)
    extreme = jax.random.randint(pick_key, (), 0, 3)
    index = jnp.where(jnp.arange(COMPS) == spot, extreme, index)
    return (BASE + jnp.take(table, index, axis=0)).astype(jnp.int32)


def draw_comp_coefs(key, part):
    key = jax.random.fold_in(key, 23)
    size_key, sign_key, order_key = jax.random.split(key, 3)
    magnitude = jax.random.randint(size_key, (COMPS,), 1, 3)
    signs = 2 * jax.random.randint(sign_key, (COMPS,), 0, 2) - 1
    values = magnitude * signs
    order = jax.random.permutation(order_key, COMPS)
    values = values.at[order[0]].set(-2).at[order[1]].set(2)
    return values.astype(jnp.int32)


def shard_levels(own_key, extent, cuts, least, top_value):
    loudness = 1.0
    for dim, shards_of in cuts:
        steps = jax.random.uniform(jax.random.fold_in(jax.random.fold_in(own_key, 6), dim), (shards_of,), jnp.float32, least / len(cuts), top_value / len(cuts))
        loudness = loudness * jnp.repeat(jnp.exp(steps), extent[dim] // shards_of).reshape((-1,) + (1,) * (len(extent) - 1 - dim))
    return loudness


def normal_values(key, dims, scale, most, cuts=(), kind=jnp.bfloat16):
    values = jax.random.normal(key, dims, jnp.float32) * scale
    if len(cuts) > 0:
        values = shard_levels(key, dims, cuts, -0.22, 0.18) * values
    return jnp.clip(values, min=-most, max=most).astype(kind)


def setup_inputs(seed: int = 0) -> dict:
    key_of = jax.random.split(jax.random.key(seed), 5)
    return {
        "modal_coefs": normal_values(key_of[0], (COMPS, CELLS0, GRID, COEF), 1.0, 6.0, ((0, 16), (1, 16)), jnp.float32),
        "comp_levels": draw_comp_levels(jax.random.fold_in(key_of[4], 71), 0),
        "comp_coefs": draw_comp_coefs(jax.random.fold_in(key_of[4], 71), 0),
        "velocity": jnp.clip(jnp.exp(jax.random.uniform(key_of[3], (4,), jnp.float32, math.log(0.5), math.log(2.0))), 0.5, 2.0),
    }


courant = 0.1
highest = lax.Precision.HIGHEST

def legendre(order, points):
    values = np.asarray(points) * 1.0
    if order == 0:
        poly = values * 0.0 + 1.0
    elif order == 1:
        poly = values
    elif order == 2:
        poly = (3.0 * values * values - 1.0) / 2.0
    else:
        poly = (5.0 * values * values * values - 3.0 * values) / 2.0
    return np.sqrt((2 * order + 1) / 2.0) * poly

def line_tables():
    nodes = np.array([-0.8611363115940526, -0.3399810435848563, 0.3399810435848563, 0.8611363115940526])
    weights = np.array([0.3478548451374538, 0.6521451548625461, 0.6521451548625461, 0.3478548451374538])
    stiff = np.zeros((4, 4))
    coarse = np.zeros((4, 8))
    for row in range(4):
        for column in range(4):
            if column < row and (row + column) % 2 == 1:
                stiff[row, column] = np.sqrt((2.0 * row + 1.0) * (2.0 * column + 1.0))
            coarse[row, column] = np.sum(weights * legendre(row, (nodes - 1.0) / 2.0) * legendre(column, nodes)) / np.sqrt(2.0)
            coarse[row, column + 4] = np.sum(weights * legendre(row, (nodes + 1.0) / 2.0) * legendre(column, nodes)) / np.sqrt(2.0)
    right = np.array([float(legendre(order, 1.0)) for order in range(4)])
    left = np.array([float(legendre(order, -1.0)) for order in range(4)])
    rows = [coarse[index] for index in range(4)]
    for index in range(4, 8):
        vector = np.eye(8)[index]
        for other in rows:
            vector = vector - np.dot(other, vector) * other
        rows.append(vector / np.sqrt(np.sum(vector * vector)))
    return (stiff - np.outer(right, right), right, left, np.array(rows))

def along(matrix, axis):
    return np.kron(np.eye(4 ** axis), np.kron(matrix, np.eye(4 ** (3 - axis))))

def pair_matrix(filters, axis):
    upper = np.concatenate([along(filters[:4, :4], axis), along(filters[:4, 4:], axis)], axis=1)
    lower = np.concatenate([along(filters[4:, :4], axis), along(filters[4:, 4:], axis)], axis=1)
    return np.concatenate([upper, lower], axis=0)

def operator_tables():
    interior, right, left, filters = line_tables()
    stiff_terms = jnp.asarray(np.stack([along(interior, axis) for axis in range(4)]), dtype=jnp.float32)
    trace_rows = jnp.asarray(np.concatenate([along(right[None, :], axis) for axis in range(4)], axis=0), dtype=jnp.float32)
    lift_cols = jnp.asarray(np.stack([along(left[:, None], axis) for axis in range(4)]), dtype=jnp.float32)
    pair_maps = jnp.asarray(np.stack([pair_matrix(filters, axis) for axis in (1, 2, 3)]), dtype=jnp.float32)
    return (stiff_terms, trace_rows, lift_cols, pair_maps)

def valid_codes():
    span = 2 ** RISE
    heights = [int(value).bit_length() for value in range(span)]
    return np.array([(one * span + two) * span + three for one in range(span) for two in range(span) for three in range(span) if heights[one] + heights[two] + heights[three] <= RISE], dtype=np.int32)

def grid_geometry(levels):
    sizes = jnp.left_shift(jnp.int32(1), levels.astype(jnp.int32))
    strides = [sizes[1] * sizes[2], sizes[2], jnp.int32(1)]
    cells = jnp.arange(GRID, dtype=jnp.int32)
    coords = [cells // strides[axis] % sizes[axis] for axis in range(3)]
    return (sizes, strides, coords)

def grid_back(values, stride, count, coord):
    behind = jnp.roll(values, stride, axis=1)
    wrapped = jnp.roll(values, stride - count * stride, axis=1)
    return jnp.where((coord == 0)[None, :, None], wrapped, behind)

def slope(field, scales, geometry, tables):
    stiff_terms, trace_rows, lift_cols = tables
    sizes, strides, coords = geometry
    volume_matrix = sum((scales[axis] * stiff_terms[axis] for axis in range(4)))
    lift_matrix = jnp.concatenate([scales[axis] * lift_cols[axis] for axis in range(4)], axis=1)
    volume = jnp.dot(field, volume_matrix.T, precision=highest, preferred_element_type=jnp.float32)
    traces = jnp.dot(field, trace_rows.T, precision=highest, preferred_element_type=jnp.float32)
    block = jnp.arange(traces.shape[2], dtype=jnp.int32) // (traces.shape[2] // 4)
    shifted = jnp.roll(traces, 1, axis=0)
    for axis in range(3):
        moved = grid_back(traces, strides[axis], sizes[axis], coords[axis])
        shifted = jnp.where(block == axis + 1, moved, shifted)
    return volume + jnp.dot(shifted, lift_matrix.T, precision=highest, preferred_element_type=jnp.float32)

def pair_cells(stride, count, level_step):
    half = GRID >> level_step + 1
    index = jnp.arange(half, dtype=jnp.int32)
    inner = index % stride
    rest = index // stride
    runs = jnp.maximum(jnp.right_shift(count, level_step + 1), 1)
    first = rest // runs * (count * stride) + rest % runs * (stride * 2 ** (level_step + 1)) + inner
    return (first, first + stride * 2 ** level_step)

def level_pass(field, pair_map, stride, count, level_step, active, inverse):

    def apply(values):
        first, second = pair_cells(stride, count, level_step)
        joined = jnp.concatenate([jnp.take(values, first, axis=1), jnp.take(values, second, axis=1)], axis=2)
        matrix = pair_map if inverse else pair_map.T
        mixed = jnp.dot(joined, matrix, precision=highest, preferred_element_type=jnp.float32)
        width = values.shape[2]
        return values.at[:, first].set(mixed[:, :, :width]).at[:, second].set(mixed[:, :, width:])

    def keep(values):
        return values
    return lax.cond(active, apply, keep, field)

def hierarchize(field, levels, geometry, pair_maps, inverse):
    sizes, strides, coords = geometry
    rises = levels - BASE
    order = [(axis, level_step) for axis in range(3) for level_step in range(RISE)]
    if inverse:
        order = order[::-1]
    for axis, level_step in order:
        field = level_pass(field, pair_maps[axis], strides[axis], sizes[axis], level_step, level_step < rises[axis], inverse)
    return field

def piece_layout(levels):
    rises = levels - BASE
    sizes, strides, coords = grid_geometry(levels)
    side = 2 ** BASE
    pieces = jnp.zeros(GRID, jnp.int32)
    inner = jnp.zeros(GRID, jnp.int32)
    for axis in range(3):
        coord = coords[axis]
        rise = rises[axis]
        low = coord % jnp.left_shift(jnp.int32(1), rise)
        run = sum(((low % 2 ** (bit + 1) == 0).astype(jnp.int32) for bit in range(RISE)))
        height = rise - run
        above = jnp.right_shift(coord, run + 1)
        detail_piece = jnp.left_shift(jnp.int32(1), jnp.maximum(height - 1, 0)) + jnp.right_shift(above, BASE)
        is_base = low == 0
        local_piece = jnp.where(is_base, 0, detail_piece)
        local_place = jnp.where(is_base, jnp.right_shift(coord, rise), above % side)
        pieces = pieces * jnp.left_shift(jnp.int32(1), rise) + local_piece
        inner = inner * side + local_place
    return (pieces * side ** 3 + inner).astype(jnp.int32)

def piece_codes(levels):
    rises = levels - BASE
    rest = jnp.arange(2 ** RISE, dtype=jnp.int32)
    digits = []
    for axis in (2, 1, 0):
        digits.append(rest % jnp.left_shift(jnp.int32(1), rises[axis]))
        rest = jnp.right_shift(rest, rises[axis])
    third, second, first = digits
    return ((first * 2 ** RISE + second) * 2 ** RISE + third, (first, second, third))

def piece_ranks(codes, valid):
    return lax.optimization_barrier(jnp.sum(jnp.where(codes[:, None] == valid[None, :], jnp.arange(valid.shape[0], dtype=jnp.int32)[None, :], 0), axis=1)).astype(jnp.int32)

def reference(modal_coefs, comp_levels, comp_coefs, velocity):
    stiff_terms, trace_rows, lift_cols, pair_maps = operator_tables()
    tables = (stiff_terms, trace_rows, lift_cols)
    sizes_all = jnp.left_shift(jnp.int32(1), comp_levels)
    reach = velocity[0] * CELLS0 + lax.optimization_barrier(jnp.sum(velocity[1:][None, :] * sizes_all.astype(jnp.float32), axis=1))
    step_size = courant / jnp.max(reach)
    valid = jnp.asarray(valid_codes())
    places = (2 ** BASE) ** 3

    def advance(inputs):
        field, levels = inputs
        geometry = grid_geometry(levels)
        scales = 2.0 * velocity * jnp.concatenate([jnp.full((1,), CELLS0, jnp.float32), geometry[0].astype(jnp.float32)])
        section = field + step_size * slope(field, scales, geometry, tables)
        advanced = 0.5 * field + 0.5 * (section + step_size * slope(section, scales, geometry, tables))
        hier = hierarchize(advanced, levels, geometry, pair_maps, False)
        position = piece_layout(levels)
        order = jnp.zeros(GRID, jnp.int32).at[position].set(jnp.arange(GRID, dtype=jnp.int32))
        return jnp.take(hier, order, axis=1).reshape(CELLS0, 2 ** RISE, places, COEF)
    pieces = lax.map(advance, (modal_coefs, comp_levels))

    def rank_one(levels):
        return piece_ranks(piece_codes(levels)[0], valid)
    ranks = jax.vmap(rank_one)(comp_levels)
    total = jnp.zeros((valid.shape[0], CELLS0, places, COEF), jnp.float32)

    def accumulate(carry, inputs):
        piece_set, rank_set, weight = inputs
        return (carry.at[rank_set].add(weight.astype(jnp.float32) * jnp.moveaxis(piece_set, 1, 0)), jnp.float32(0.0))
    total = lax.scan(accumulate, total, (pieces, ranks, comp_coefs))[0]

    def restore(inputs):
        levels, rank_set = inputs
        geometry = grid_geometry(levels)
        gathered = jnp.moveaxis(jnp.take(total, rank_set, axis=0), 0, 1).reshape(CELLS0, GRID, COEF)
        position = piece_layout(levels)
        hier = jnp.take(gathered, position, axis=1)
        return hierarchize(hier, levels, geometry, pair_maps, True)
    return lax.map(restore, (comp_levels, ranks))
```

```python
import functools

import jax
import jax.numpy as jnp
import ml_dtypes
import numpy as np
from jax import lax
from jax.experimental import pallas as pl
from jax.experimental.pallas import tpu as pltpu
from jax.sharding import PartitionSpec as P

COEF = 256
BASE = 2
RISE = 3
GRID = 512
LOW = 2**RISE
PLACES = (2**BASE) ** 3
KINDS = (RISE + 1) * (RISE + 2) // 2
BF16 = jnp.bfloat16
F32 = jnp.float32
MESH = pl.DeviceIdType.MESH

courant = 0.1


def legendre(order, points):
    values = np.asarray(points) * 1.0
    if order == 0:
        poly = values * 0.0 + 1.0
    elif order == 1:
        poly = values
    elif order == 2:
        poly = (3.0 * values * values - 1.0) / 2.0
    else:
        poly = (5.0 * values * values * values - 3.0 * values) / 2.0
    return np.sqrt((2 * order + 1) / 2.0) * poly


def line_tables():
    nodes = np.array(
        [-0.8611363115940526, -0.3399810435848563, 0.3399810435848563, 0.8611363115940526]
    )
    weights = np.array(
        [0.3478548451374538, 0.6521451548625461, 0.6521451548625461, 0.3478548451374538]
    )
    stiff = np.zeros((4, 4))
    coarse = np.zeros((4, 8))
    for row in range(4):
        for column in range(4):
            if column < row and (row + column) % 2 == 1:
                stiff[row, column] = np.sqrt((2.0 * row + 1.0) * (2.0 * column + 1.0))
            coarse[row, column] = np.sum(
                weights * legendre(row, (nodes - 1.0) / 2.0) * legendre(column, nodes)
            ) / np.sqrt(2.0)
            coarse[row, column + 4] = np.sum(
                weights * legendre(row, (nodes + 1.0) / 2.0) * legendre(column, nodes)
            ) / np.sqrt(2.0)
    right = np.array([float(legendre(order, 1.0)) for order in range(4)])
    left = np.array([float(legendre(order, -1.0)) for order in range(4)])
    rows = [coarse[index] for index in range(4)]
    for index in range(4, 8):
        vector = np.eye(8)[index]
        for other in rows:
            vector = vector - np.dot(other, vector) * other
        rows.append(vector / np.sqrt(np.sum(vector * vector)))
    return (stiff - np.outer(right, right), right, left, np.array(rows))


def along(matrix, axis):
    return np.kron(np.eye(4**axis), np.kron(matrix, np.eye(4 ** (3 - axis))))


def split_table(table):
    hi = table.astype(ml_dtypes.bfloat16)
    lo = (table - hi.astype(np.float64)).astype(ml_dtypes.bfloat16)
    return np.stack([hi, lo], axis=-3)


def line_hierarchy(filters, rise):
    cells = 2**rise
    whole = np.eye(cells * 4).reshape(cells, 4, cells * 4)
    for level_step in range(rise):
        for first in range(0, cells, 2 ** (level_step + 1)):
            second = first + 2**level_step
            pair = np.concatenate([whole[first], whole[second]], axis=0)
            mixed = filters @ pair
            whole[first], whole[second] = mixed[:4], mixed[4:]
    ordered = np.zeros_like(whole)
    for low in range(cells):
        digit = 0
        if low > 0:
            zeros = (low & -low).bit_length() - 1
            height = rise - zeros
            digit = 2 ** (height - 1) + (low >> (zeros + 1))
        ordered[digit] = whole[low]
    return ordered.reshape(cells, 4, cells, 4)


def compositions():
    return [(a, b, RISE - a - b) for a in range(RISE + 1) for b in range(RISE + 1 - a)]


@functools.lru_cache(None)
def tables():
    interior, right, left, filters = line_tables()
    stiff = np.stack([along(interior, axis).T for axis in range(4)]).astype(np.float32)
    lift = np.concatenate([along(left[:, None], axis).T for axis in range(4)]).astype(np.float32)
    trace = np.concatenate([along(right[None, :], axis) for axis in range(4)], axis=0).T
    lines = [line_hierarchy(filters, rise) for rise in range(RISE + 1)]
    hier = []
    for one, two, three in compositions():
        whole = np.einsum("aqlp,brms,cuno->qruabclmnpso", lines[one], lines[two], lines[three])
        hier.append(whole.reshape(GRID, GRID))
    return stiff, lift, split_table(trace), split_table(np.stack(hier))


def split(values):
    hi = values.astype(BF16)
    return hi, (values - hi.astype(F32)).astype(BF16)


def dot(one, two):
    return jnp.dot(one, two, preferred_element_type=F32)


def dot_nt(one, two):
    return lax.dot_general(one, two, (((1,), (1,)), ((), ())), preferred_element_type=F32)


def kernel(
    comps,
    shards,
    levels,
    coefs,
    velocity,
    x_hbm,
    stiff_hbm,
    lift_hbm,
    trace_hbm,
    hier_hbm,
    out_hbm,
    x_v,
    stiff_v,
    lift_v,
    trace_v,
    hier_v,
    onehot,
    match,
    wide,
    lifts,
    field,
    traces1,
    traces2,
    shifted,
    section,
    edge_out,
    edge_in,
    rows,
    sent,
    got,
    back,
    home,
    local_sem,
    edge_send,
    edge_recv,
    there_send,
    there_recv,
    back_send,
    back_recv,
):
    me = lax.axis_index("comp")
    spot = lax.axis_index("shard")
    ahead = lax.rem(spot + 1, shards)
    behind = lax.rem(spot + shards - 1, shards)

    x_copy = pltpu.make_async_copy(x_hbm.at[0, 0], x_v, local_sem.at[0])
    trace_copy = pltpu.make_async_copy(trace_hbm, trace_v, local_sem.at[1])
    stiff_copy = pltpu.make_async_copy(stiff_hbm, stiff_v, local_sem.at[2])
    lift_copy = pltpu.make_async_copy(lift_hbm, lift_v, local_sem.at[3])
    hier_copy = pltpu.make_async_copy(hier_hbm, hier_v, local_sem.at[4])
    x_copy.start()
    stiff_copy.start()
    lift_copy.start()
    trace_copy.start()
    hier_copy.start()

    barrier = pltpu.get_barrier_semaphore()
    others = [lax.rem(me + step, comps) for step in range(1, comps)]
    for other in others:
        pl.semaphore_signal(barrier, inc=1, device_id={"comp": other}, device_id_type=MESH)
    pl.semaphore_signal(barrier, inc=1, device_id={"shard": ahead}, device_id_type=MESH)
    pl.semaphore_signal(barrier, inc=1, device_id={"shard": behind}, device_id_type=MESH)

    def rise_of(comp, axis):
        return jnp.clip(levels[comp, axis] - BASE, 0, RISE)

    rise1 = rise_of(me, 0)
    rise2 = rise_of(me, 1)
    rise3 = rise_of(me, 2)
    kind = jnp.clip(lax.shift_right_logical(rise1 * (9 - rise1), 1) + rise2, 0, KINDS - 1)
    one = jnp.int32(1)
    reach = None
    for comp in range(comps):
        total = velocity[0] * (1.0 * shards)
        for axis in range(3):
            size = lax.shift_left(one, levels[comp, axis]).astype(F32)
            total = total + velocity[axis + 1] * size
        reach = total if reach is None else jnp.maximum(reach, total)
    step_size = jnp.full((1, COEF), courant, F32) / jnp.full((1, COEF), reach, F32)
    sizes = [jnp.float32(shards)] + [
        lax.shift_left(one, levels[me, axis]).astype(F32) for axis in range(3)
    ]
    scales = [step_size * (2.0 * velocity[axis] * sizes[axis]) for axis in range(4)]

    def low_digits(low):
        low3 = low & (lax.shift_left(one, rise3) - 1)
        low2 = lax.shift_right_logical(low, rise3) & (lax.shift_left(one, rise2) - 1)
        low1 = lax.shift_right_logical(low, rise2 + rise3)
        return low1, low2, low3

    def cell_of(digit1, digit2, digit3):
        return (
            lax.shift_left(digit1, rise2 + rise3 + 2 * BASE)
            + lax.shift_left(digit2, rise3 + BASE)
            + digit3
        )

    offsets = [cell_of(*low_digits(jnp.int32(low))) for low in range(LOW)]

    def place_cell(place):
        return cell_of(
            lax.shift_left(lax.shift_right_logical(place, 4) & 3, jnp.full(place.shape, rise1)),
            lax.shift_left(lax.shift_right_logical(place, 2) & 3, jnp.full(place.shape, rise2)),
            lax.shift_left(place & 3, jnp.full(place.shape, rise3)),
        )

    place_rows = place_cell(lax.broadcasted_iota(jnp.int32, (PLACES, 128), 0))
    lanes = lax.broadcasted_iota(jnp.int32, (PLACES, 128), 1)
    for low in range(LOW):
        for part in range(GRID // 128):
            hit = (place_rows + offsets[low]) == (lanes + 128 * part)
            onehot[low * PLACES : (low + 1) * PLACES, 128 * part : 128 * (part + 1)] = jnp.where(
                hit, 1.0, 0.0
            ).astype(BF16)

    stiff_copy.wait()
    volume = scales[0] * stiff_v[0]
    for axis in range(1, 4):
        volume = volume + scales[axis] * stiff_v[axis]
    wide[0], wide[1] = split(volume)
    lift_copy.wait()
    for axis in range(4):
        rows_of = slice(64 * axis, 64 * (axis + 1))
        hi, lo = split(scales[axis] * lift_v[rows_of, :])
        lifts[0, rows_of, :] = hi
        lifts[1, rows_of, :] = lo

    x_copy.wait()
    hi, lo = split(x_v[...])
    field[...] = dot(onehot[...], hi) + dot(onehot[...], lo)

    left_half = lax.broadcasted_iota(jnp.int32, (PLACES, 128), 1) < 64
    place_row = lax.broadcasted_iota(jnp.int32, (PLACES, 128), 0)

    def halves(one, two):
        return jnp.where(left_half, one, two)

    def swap(values):
        return pltpu.roll(values, 64, 1)

    def behind_of(low, axis):
        digits = list(low_digits(jnp.int32(low)))
        rise = (rise1, rise2, rise3)[axis]
        first = digits[axis] == 0
        digits[axis] = (digits[axis] + lax.shift_left(one, rise) - 1) & (
            lax.shift_left(one, rise) - 1
        )
        spot = (
            lax.shift_left(digits[0], rise2 + rise3) + lax.shift_left(digits[1], rise3) + digits[2]
        )
        return spot & (LOW - 1), first

    sources = []
    for low in range(LOW):
        spot1, first1 = behind_of(low, 0)
        spot2, first2 = behind_of(low, 1)
        spot3, first3 = behind_of(low, 2)
        sources.append(
            (
                spot1 + jnp.where(first1, LOW, 0),
                spot2 + jnp.where(first2, LOW, 0),
                spot3 + jnp.where(first3, 2 * LOW, 0),
            )
        )

    trace_copy.wait()

    def slope_step(hi, lo, stage, after_start):
        trace = (
            dot(hi, trace_v[0]) + dot(lo, trace_v[0]) + dot(hi, trace_v[1])
        ).reshape(LOW, PLACES, COEF)
        t01, t23 = trace[:, :, :128], trace[:, :, 128:]
        for low in range(LOW // 2):
            edge_out[stage, low] = halves(t01[low], swap(t01[low + LOW // 2]))
        after_start()
        copy = pltpu.make_async_remote_copy(
            src_ref=edge_out.at[stage],
            dst_ref=edge_in.at[stage],
            send_sem=edge_send.at[stage],
            recv_sem=edge_recv.at[stage],
            device_id={"shard": ahead},
            device_id_type=MESH,
        )
        copy.start()
        for low in range(LOW):
            traces1[low] = t01[low]
            traces1[LOW + low] = pltpu.roll(t01[low], 16, 0)
            now = t23[low]
            traces2[low] = now
            traces2[LOW + low] = jnp.where(
                (place_row & 15) < 4, pltpu.roll(now, PLACES - 12, 0), pltpu.roll(now, 4, 0)
            )
            traces2[2 * LOW + low] = jnp.where(
                (place_row & 3) < 1, pltpu.roll(now, PLACES - 3, 0), pltpu.roll(now, 1, 0)
            )
        inner = dot(hi, wide[0]) + dot(lo, wide[0]) + dot(hi, wide[1])
        copy.wait()
        for low in range(LOW):
            edge = edge_in[stage, low % (LOW // 2)]
            if low >= LOW // 2:
                edge = swap(edge)
            from1, from2, from3 = sources[low]
            rows_of = slice(low * PLACES, (low + 1) * PLACES)
            shifted[rows_of, :128] = halves(edge, traces1[from1])
            shifted[rows_of, 128:] = halves(traces2[from2], traces2[from3])
        s_hi, s_lo = split(shifted[...])
        return inner + (dot(s_hi, lifts[0]) + dot(s_lo, lifts[0]) + dot(s_hi, lifts[1]))

    def wait_barrier():
        pl.semaphore_wait(barrier, comps + 1)

    hi, lo = split(field[...])
    section[...] = field[...] + slope_step(hi, lo, 0, wait_barrier)
    hi, lo = split(section[...])
    section[...] = 0.5 * field[...] + 0.5 * (
        section[...] + slope_step(hi, lo, 1, lambda: None)
    )

    for pair in range(LOW // 2):
        for group in range(2):
            columns = slice(128 * group, 128 * (group + 1))
            even = section[2 * pair * PLACES : (2 * pair + 1) * PLACES, columns]
            odd = section[(2 * pair + 1) * PLACES : (2 * pair + 2) * PLACES, columns]
            for half, block in ((0, halves(even, swap(odd))), (1, halves(swap(even), odd))):
                top = (2 * group + half) * PLACES
                hi, lo = split(block)
                rows[0, top : top + PLACES, 128 * pair : 128 * (pair + 1)] = hi
                rows[1, top : top + PLACES, 128 * pair : 128 * (pair + 1)] = lo

    hier_copy.wait()
    h_hi, h_lo = hier_v[kind, 0], hier_v[kind, 1]
    hier = dot_nt(h_hi, rows[0]) + dot_nt(h_hi, rows[1]) + dot_nt(h_lo, rows[0])
    sent[...] = hier.reshape(sent.shape)

    def exchange(source, target, send_sem, recv_sem):
        copies = []
        for step in (8, 4, 12, 5, 11, 3, 13, 6, 10, 2, 14, 7, 9, 1, 15):
            other = lax.rem(me + step, comps)
            copy = pltpu.make_async_remote_copy(
                src_ref=source.at[other],
                dst_ref=target.at[me],
                send_sem=send_sem.at[step],
                recv_sem=recv_sem.at[step],
                device_id={"comp": other},
                device_id_type=MESH,
            )
            copy.start()
            copies.append(copy)
        target[me] = source[me]
        return copies

    copies = exchange(sent, got, there_send, there_recv)

    def code_of(digits, comp):
        up2 = rise_of(comp, 1)
        up3 = rise_of(comp, 2)
        digit3 = digits & (lax.shift_left(one, up3) - 1)
        digit2 = lax.shift_right_logical(digits, jnp.full(digits.shape, up3)) & (
            lax.shift_left(one, up2) - 1
        )
        digit1 = lax.shift_right_logical(digits, jnp.full(digits.shape, up2 + up3))
        return digit1 * 64 + digit2 * 8 + digit3

    piece_row = lax.broadcasted_iota(jnp.int32, (8, 128), 0)
    piece_lane = lax.broadcasted_iota(jnp.int32, (8, 128), 1)
    lane_code = jnp.zeros((8, 128), jnp.int32)
    lane_coef = jnp.zeros((8, 128), F32)
    for comp in range(comps):
        own = lax.shift_right_logical(piece_lane, 3) == comp
        lane_code = jnp.where(own, code_of(piece_lane & 7, comp), lane_code)
        lane_coef = jnp.where(own, jnp.full((8, 128), coefs[comp].astype(F32)), lane_coef)
    for comp in range(0, comps, 2):
        block = [
            jnp.where(code_of(piece_row, here) == lane_code, lane_coef, 0.0)
            for here in (comp, comp + 1)
        ]
        match[8 * comp : 8 * comp + 16, :] = jnp.concatenate(block, axis=0).astype(BF16)

    for copy in copies:
        copy.wait()
    for quarter in range(4):
        part = slice(8 * quarter, 8 * (quarter + 1))
        hi, lo = split(got[:, part, :].reshape(8 * comps, COEF))
        total = dot(match[...], hi) + dot(match[...], lo)
        back[:, part, :] = total.reshape(comps, 8, COEF)
    copies = exchange(back, home, back_send, back_recv)

    cell_rows = lax.broadcasted_iota(jnp.int32, (GRID, 128), 0)
    lane = lax.broadcasted_iota(jnp.int32, (8, 128), 1)
    lane_place = place_cell(lane & (PLACES - 1))
    for part in range(GRID // 128):
        lane_cell = lane_place + jnp.where(lane < 64, offsets[2 * part], offsets[2 * part + 1])
        onehot[:, 128 * part : 128 * (part + 1)] = jnp.where(
            cell_rows == lane_cell[0:1, :], 1.0, 0.0
        ).astype(BF16)

    for copy in copies:
        copy.wait()
    hi, lo = split(home[...].reshape(GRID, COEF).T)
    plain = dot(hi, h_hi) + dot(lo, h_hi) + dot(hi, h_lo)
    for pair in range(LOW // 2):
        for group in range(2):
            columns = slice(128 * group, 128 * (group + 1))
            one_block = plain[
                2 * group * PLACES : (2 * group + 1) * PLACES, 128 * pair : 128 * (pair + 1)
            ]
            two_block = plain[
                (2 * group + 1) * PLACES : (2 * group + 2) * PLACES, 128 * pair : 128 * (pair + 1)
            ]
            section[2 * pair * PLACES : (2 * pair + 1) * PLACES, columns] = halves(
                one_block, swap(two_block)
            )
            section[(2 * pair + 1) * PLACES : (2 * pair + 2) * PLACES, columns] = halves(
                swap(one_block), two_block
            )
    hi, lo = split(section[...])
    x_v[...] = dot(onehot[...], hi) + dot(onehot[...], lo)
    out_copy = pltpu.make_async_copy(x_v, out_hbm.at[0, 0], local_sem.at[0])
    out_copy.start()
    out_copy.wait()


def on_device(modal_coefs, comp_levels, comp_coefs, velocity):
    comps = lax.axis_size("comp")
    shards = lax.axis_size("shard")
    stiff, lift, trace, hier = tables()
    smem = pl.BlockSpec(memory_space=pltpu.SMEM)
    anywhere = pl.BlockSpec(memory_space=pl.ANY)
    dma = pltpu.SemaphoreType.DMA
    exchanged = pltpu.VMEM((comps, GRID // comps, COEF), F32)
    return pl.pallas_call(
        functools.partial(kernel, comps, shards),
        out_shape=jax.ShapeDtypeStruct(modal_coefs.shape, F32),
        in_specs=[smem] * 3 + [anywhere] * 5,
        out_specs=anywhere,
        scratch_shapes=[
            pltpu.VMEM((GRID, COEF), F32),
            pltpu.VMEM(stiff.shape, F32),
            pltpu.VMEM(lift.shape, F32),
            pltpu.VMEM(trace.shape, BF16),
            pltpu.VMEM(hier.shape, BF16),
            pltpu.VMEM((GRID, GRID), BF16),
            pltpu.VMEM((8 * comps, 8 * comps), BF16),
            pltpu.VMEM((2, COEF, COEF), BF16),
            pltpu.VMEM((2, COEF, COEF), BF16),
            pltpu.VMEM((GRID, COEF), F32),
            pltpu.VMEM((2 * LOW, PLACES, 128), F32),
            pltpu.VMEM((3 * LOW, PLACES, 128), F32),
            pltpu.VMEM((GRID, COEF), F32),
            pltpu.VMEM((GRID, COEF), F32),
            pltpu.VMEM((2, LOW // 2, PLACES, 128), F32),
            pltpu.VMEM((2, LOW // 2, PLACES, 128), F32),
            pltpu.VMEM((2, COEF, GRID), BF16),
            exchanged,
            exchanged,
            exchanged,
            exchanged,
            dma((5,)),
            dma((2,)),
            dma((2,)),
            dma((comps,)),
            dma((comps,)),
            dma((comps,)),
            dma((comps,)),
        ],
        compiler_params=pltpu.CompilerParams(
            collective_id=0, has_side_effects=True, vmem_limit_bytes=48 * 2**20
        ),
        name="combine",
    )(
        comp_levels,
        comp_coefs,
        velocity,
        modal_coefs,
        jnp.asarray(stiff),
        jnp.asarray(lift),
        jnp.asarray(trace),
        jnp.asarray(hier),
    )


def solution(mesh):
    placed = (P("comp", "shard", None, None), P(), P(), P())
    return jax.shard_map(
        on_device,
        mesh=mesh,
        in_specs=placed,
        out_specs=P("comp", "shard", None, None),
        check_vma=False,
    )
```

```python
import functools

import jax
import jax.numpy as jnp
import ml_dtypes
import numpy as np
from jax import lax
from jax.experimental import pallas as pl
from jax.experimental.pallas import tpu as pltpu
from jax.sharding import PartitionSpec as P

COEF = 256
BASE = 2
RISE = 3
GRID = 512
LOW = 2**RISE
PLACES = (2**BASE) ** 3
KINDS = (RISE + 1) * (RISE + 2) // 2
BF16 = jnp.bfloat16
F32 = jnp.float32
MESH = pl.DeviceIdType.MESH

courant = 0.1
VMEM_LIMIT = 62 * 2**20
ORDER = (8, 4, 12, 5, 11, 3, 13, 6, 10, 2, 14, 7, 9, 1, 15)
LEFT = [float((-1) ** order * np.sqrt((2 * order + 1) / 2.0)) for order in range(4)]
RIGHT_LEFT = float(sum((-1) ** order * (2 * order + 1) / 2.0 for order in range(4)))


def legendre(order, points):
    values = np.asarray(points) * 1.0
    if order == 0:
        poly = values * 0.0 + 1.0
    elif order == 1:
        poly = values
    elif order == 2:
        poly = (3.0 * values * values - 1.0) / 2.0
    else:
        poly = (5.0 * values * values * values - 3.0 * values) / 2.0
    return np.sqrt((2 * order + 1) / 2.0) * poly


def line_tables():
    nodes = np.array(
        [-0.8611363115940526, -0.3399810435848563, 0.3399810435848563, 0.8611363115940526]
    )
    weights = np.array(
        [0.3478548451374538, 0.6521451548625461, 0.6521451548625461, 0.3478548451374538]
    )
    stiff = np.zeros((4, 4))
    coarse = np.zeros((4, 8))
    for row in range(4):
        for column in range(4):
            if column < row and (row + column) % 2 == 1:
                stiff[row, column] = np.sqrt((2.0 * row + 1.0) * (2.0 * column + 1.0))
            coarse[row, column] = np.sum(
                weights * legendre(row, (nodes - 1.0) / 2.0) * legendre(column, nodes)
            ) / np.sqrt(2.0)
            coarse[row, column + 4] = np.sum(
                weights * legendre(row, (nodes + 1.0) / 2.0) * legendre(column, nodes)
            ) / np.sqrt(2.0)
    right = np.array([float(legendre(order, 1.0)) for order in range(4)])
    left = np.array([float(legendre(order, -1.0)) for order in range(4)])
    rows = [coarse[index] for index in range(4)]
    for index in range(4, 8):
        vector = np.eye(8)[index]
        for other in rows:
            vector = vector - np.dot(other, vector) * other
        rows.append(vector / np.sqrt(np.sum(vector * vector)))
    return (stiff - np.outer(right, right), right, left, np.array(rows))


def along(matrix, axis):
    return np.kron(np.eye(4**axis), np.kron(matrix, np.eye(4 ** (3 - axis))))


def split_table(table):
    hi = table.astype(ml_dtypes.bfloat16)
    lo = (table - hi.astype(np.float64)).astype(ml_dtypes.bfloat16)
    return np.stack([hi, lo], axis=-3)


def line_hierarchy(filters, rise):
    cells = 2**rise
    whole = np.eye(cells * 4).reshape(cells, 4, cells * 4)
    for level_step in range(rise):
        for first in range(0, cells, 2 ** (level_step + 1)):
            second = first + 2**level_step
            pair = np.concatenate([whole[first], whole[second]], axis=0)
            mixed = filters @ pair
            whole[first], whole[second] = mixed[:4], mixed[4:]
    ordered = np.zeros_like(whole)
    for low in range(cells):
        digit = 0
        if low > 0:
            zeros = (low & -low).bit_length() - 1
            height = rise - zeros
            digit = 2 ** (height - 1) + (low >> (zeros + 1))
        ordered[digit] = whole[low]
    return ordered.reshape(cells, 4, cells, 4)


def compositions():
    return [(a, b, RISE - a - b) for a in range(RISE + 1) for b in range(RISE + 1 - a)]


@functools.lru_cache(None)
def tables():
    interior, right, left, filters = line_tables()
    stiff = np.stack([along(interior, axis).T for axis in range(4)]).astype(np.float32)
    lift = np.concatenate([along(left[:, None], axis).T for axis in range(4)]).astype(np.float32)
    trace = np.concatenate([along(right[None, :], axis) for axis in range(4)], axis=0).T
    lines = [line_hierarchy(filters, rise) for rise in range(RISE + 1)]
    hier = []
    for one, two, three in compositions():
        whole = np.einsum("aqlp,brms,cuno->qruabclmnpso", lines[one], lines[two], lines[three])
        hier.append(whole.reshape(GRID, GRID))
    hi, lo = split_table(trace)
    return stiff, lift, np.concatenate([hi, hi, lo]), split_table(np.stack(hier))


def split(values):
    hi = values.astype(BF16)
    return hi, (values - hi.astype(F32)).astype(BF16)


def dot(one, two):
    return jnp.dot(one, two, preferred_element_type=F32)


def dot_nt(one, two):
    return lax.dot_general(one, two, (((1,), (1,)), ((), ())), preferred_element_type=F32)


def triple(hi, lo):
    return jnp.concatenate([hi, lo, hi], axis=1)


def kernel(
    comps,
    shards,
    levels_hbm,
    coefs_hbm,
    velocity_hbm,
    x_hbm,
    stiff_hbm,
    lift_hbm,
    trace_hbm,
    hier_hbm,
    out_ref,
    levels,
    coefs,
    velocity,
    x_v,
    stiff_v,
    lift_v,
    trace_v,
    hier_v,
    onehot,
    match,
    wide,
    lifts,
    field,
    traces1,
    traces2,
    shifted,
    section,
    edge_out,
    edge_in,
    rows,
    sent,
    got,
    back,
    home,
    local_sem,
    edge_send,
    edge_recv,
    there_send,
    there_recv,
    back_send,
    back_recv,
):
    me = lax.axis_index("comp")
    spot = lax.axis_index("shard")
    ahead = lax.rem(spot + 1, shards)
    behind = lax.rem(spot + shards - 1, shards)

    def fetch(source, target, index):
        copy = pltpu.make_async_copy(source, target, local_sem.at[index])
        copy.start()
        return copy

    levels_copy = fetch(levels_hbm, levels, 0)
    x_copy = fetch(x_hbm.at[0, 0], x_v, 1)
    velocity_copy = fetch(velocity_hbm, velocity, 2)
    trace_copy = fetch(trace_hbm, trace_v, 3)
    stiff_copy = fetch(stiff_hbm, stiff_v, 4)
    lift_copy = fetch(lift_hbm, lift_v, 5)
    coefs_copy = fetch(coefs_hbm, coefs, 6)
    hier_copy = fetch(hier_hbm, hier_v, 7)

    barrier = pltpu.get_barrier_semaphore()
    for step in range(1, comps):
        pl.semaphore_signal(
            barrier, inc=1, device_id={"comp": lax.rem(me + step, comps)}, device_id_type=MESH
        )
    pl.semaphore_signal(barrier, inc=1, device_id={"shard": ahead}, device_id_type=MESH)
    pl.semaphore_signal(barrier, inc=1, device_id={"shard": behind}, device_id_type=MESH)

    levels_copy.wait()

    def rise_of(comp, axis):
        return jnp.clip(levels[axis, comp] - BASE, 0, RISE)

    rise1 = rise_of(me, 0)
    rise2 = rise_of(me, 1)
    rise3 = rise_of(me, 2)
    kind = jnp.clip(lax.shift_right_logical(rise1 * (9 - rise1), 1) + rise2, 0, KINDS - 1)
    one = jnp.int32(1)

    def low_digits(low):
        low3 = low & (lax.shift_left(one, rise3) - 1)
        low2 = lax.shift_right_logical(low, rise3) & (lax.shift_left(one, rise2) - 1)
        low1 = lax.shift_right_logical(low, rise2 + rise3)
        return low1, low2, low3

    def cell_of(digit1, digit2, digit3):
        return (
            lax.shift_left(digit1, rise2 + rise3 + 2 * BASE)
            + lax.shift_left(digit2, rise3 + BASE)
            + digit3
        )

    offsets = [cell_of(*low_digits(jnp.int32(low))) for low in range(LOW)]

    def place_cell(place):
        return cell_of(
            lax.shift_left(lax.shift_right_logical(place, 4) & 3, jnp.full(place.shape, rise1)),
            lax.shift_left(lax.shift_right_logical(place, 2) & 3, jnp.full(place.shape, rise2)),
            lax.shift_left(place & 3, jnp.full(place.shape, rise3)),
        )

    place_row = lax.broadcasted_iota(jnp.int32, (PLACES, 128), 0)
    lanes = lax.broadcasted_iota(jnp.int32, (PLACES, 128), 1)
    left_half = lanes < 64
    place_rows = place_cell(place_row)
    for low in range(LOW):
        for part in range(GRID // 128):
            hit = (place_rows + offsets[low]) == (lanes + 128 * part)
            onehot[low * PLACES : (low + 1) * PLACES, 128 * part : 128 * (part + 1)] = jnp.where(
                hit, 1.0, 0.0
            ).astype(BF16)

    x_copy.wait()
    hi, lo = split(x_v[...])
    new_hi, new_lo = dot(onehot[...], hi), dot(onehot[...], lo)
    field[...] = new_hi + new_lo
    thrice = triple(new_hi.astype(BF16), new_lo.astype(BF16))

    def halves(one, two):
        return jnp.where(left_half, one, two)

    def swap(values):
        return pltpu.roll(values, 64, 1)

    def block_of(low):
        return slice(low * PLACES, (low + 1) * PLACES)

    def pack(values, low):
        return halves(values[block_of(low), :], swap(values[block_of(low + LOW // 2), :]))

    def send_edge(stage):
        copy = pltpu.make_async_remote_copy(
            src_ref=edge_out.at[stage],
            dst_ref=edge_in.at[stage],
            send_sem=edge_send.at[stage],
            recv_sem=edge_recv.at[stage],
            device_id={"shard": ahead},
            device_id_type=MESH,
        )
        copy.start()
        return copy

    trace_copy.wait()
    trace = dot(thrice, trace_v[...])
    for low in range(LOW // 2):
        edge_out[0, low] = pack(trace[:, :128], low)
    pl.semaphore_wait(barrier, comps + 1)
    edge_copy = send_edge(0)

    velocity_copy.wait()
    reach = None
    for comp in range(comps):
        total = velocity[0] * (1.0 * shards)
        for axis in range(3):
            size = lax.shift_left(one, levels[axis, comp]).astype(F32)
            total = total + velocity[axis + 1] * size
        reach = total if reach is None else jnp.maximum(reach, total)
    step_size = jnp.full((1, COEF), courant, F32) / jnp.full((1, COEF), reach, F32)
    sizes = [jnp.float32(shards)] + [
        lax.shift_left(one, levels[axis, me]).astype(F32) for axis in range(3)
    ]
    scales = [step_size * (2.0 * velocity[axis] * sizes[axis]) for axis in range(4)]
    stiff_copy.wait()
    volume = scales[0] * stiff_v[0]
    for axis in range(1, 4):
        volume = volume + scales[axis] * stiff_v[axis]
    hi, lo = split(volume)
    wide[:COEF], wide[COEF : 2 * COEF], wide[2 * COEF :] = hi, hi, lo
    lift_copy.wait()
    for part in range(3):
        lifts[part * COEF : part * COEF + 64, :] = jnp.zeros((64, COEF), BF16)
    for axis in range(1, 4):
        hi, lo = split(scales[axis] * lift_v[64 * axis : 64 * (axis + 1), :])
        for part, piece in enumerate((hi, hi, lo)):
            start = part * COEF + 64 * axis
            lifts[start : start + 64, :] = piece
    lift_first = [
        scales[0][:, :128] * jnp.where(left_half[:1], LEFT[2 * group], LEFT[2 * group + 1])
        for group in range(2)
    ]
    edge_factor = scales[0][:, :128] * RIGHT_LEFT

    def behind_of(low, axis):
        digits = list(low_digits(jnp.int32(low)))
        rise = (rise1, rise2, rise3)[axis]
        first = digits[axis] == 0
        digits[axis] = (digits[axis] + lax.shift_left(one, rise) - 1) & (
            lax.shift_left(one, rise) - 1
        )
        spot = (
            lax.shift_left(digits[0], rise2 + rise3) + lax.shift_left(digits[1], rise3) + digits[2]
        )
        return spot & (LOW - 1), first

    sources = []
    for low in range(LOW):
        spot1, first1 = behind_of(low, 0)
        spot2, first2 = behind_of(low, 1)
        spot3, first3 = behind_of(low, 2)
        sources.append(
            (
                spot1 + jnp.where(first1, LOW, 0),
                spot2 + jnp.where(first2, LOW, 0),
                spot3 + jnp.where(first3, 2 * LOW, 0),
            )
        )

    def inner_slope(thrice, trace):
        for low in range(LOW):
            now = trace[block_of(low), :128]
            traces1[low] = now
            traces1[LOW + low] = pltpu.roll(now, 16, 0)
            now = trace[block_of(low), 128:]
            traces2[low] = now
            traces2[LOW + low] = jnp.where(
                (place_row & 15) < 4, pltpu.roll(now, PLACES - 12, 0), pltpu.roll(now, 4, 0)
            )
            traces2[2 * LOW + low] = jnp.where(
                (place_row & 3) < 1, pltpu.roll(now, PLACES - 3, 0), pltpu.roll(now, 1, 0)
            )
        inner = dot(thrice, wide[...])
        for low in range(LOW):
            from1, from2, from3 = sources[low]
            shifted[block_of(low), :128] = traces1[from1]
            shifted[block_of(low), 128:] = halves(traces2[from2], traces2[from3])
        return inner + dot(triple(*split(shifted[...])), lifts[...])

    def add_edge(stage, factor):
        for low in range(LOW // 2):
            edge = edge_in[stage, low]
            turned = swap(edge)
            for place, both in (
                (low, halves(edge, turned)),
                (low + LOW // 2, halves(turned, edge)),
            ):
                for group in range(2):
                    columns = slice(128 * group, 128 * (group + 1))
                    section[block_of(place), columns] += (factor * lift_first[group]) * both

    section[...] = field[...] + inner_slope(thrice, trace)
    trace = dot(triple(*split(section[...])), trace_v[:, :128])
    for low in range(LOW // 2):
        edge_out[1, low] = pack(trace, low)
    edge_copy.wait()
    for low in range(LOW // 2):
        edge_out[1, low] += edge_factor * edge_in[0, low]
    edge_copy = send_edge(1)
    add_edge(0, 1.0)

    thrice = triple(*split(section[...]))
    trace = dot(thrice, trace_v[...])
    section[...] = 0.5 * field[...] + 0.5 * (section[...] + inner_slope(thrice, trace))
    edge_copy.wait()
    add_edge(1, 0.5)

    def exchange(source, target, half, send_sem, recv_sem):
        copies = []
        for step in ORDER:
            other = lax.rem(me + step, comps)
            copy = pltpu.make_async_remote_copy(
                src_ref=source.at[half, other],
                dst_ref=target.at[half, me],
                send_sem=send_sem.at[half, step],
                recv_sem=recv_sem.at[half, step],
                device_id={"comp": other},
                device_id_type=MESH,
            )
            copy.start()
            copies.append(copy)
        target[half, me] = source[half, me]
        return copies

    there = []
    for half in range(2):
        columns = slice(128 * half, 128 * (half + 1))
        for pair in range(LOW // 2):
            even = section[block_of(2 * pair), columns]
            odd = section[block_of(2 * pair + 1), columns]
            into = slice(128 * pair, 128 * (pair + 1))
            hi, lo = split(jnp.concatenate([halves(even, swap(odd)), halves(swap(even), odd)]))
            rows[half, :128, into] = hi
            rows[half, 128:, into] = lo
        if half == 0:
            hier_copy.wait()
            h_hi, h_lo = hier_v[kind, 0], hier_v[kind, 1]
        both = dot_nt(h_hi, rows[half])
        whole = both[:, :128] + both[:, 128:] + dot_nt(h_lo, rows[half, :128])
        sent[half] = whole.reshape(sent.shape[1:])
        there.append(exchange(sent, got, half, there_send, there_recv))

    coefs_copy.wait()

    def code_of(digits, comp):
        up2 = rise_of(comp, 1)
        up3 = rise_of(comp, 2)
        digit3 = digits & (lax.shift_left(one, up3) - 1)
        digit2 = lax.shift_right_logical(digits, jnp.full(digits.shape, up3)) & (
            lax.shift_left(one, up2) - 1
        )
        digit1 = lax.shift_right_logical(digits, jnp.full(digits.shape, up2 + up3))
        return digit1 * 64 + digit2 * 8 + digit3

    piece_row = lax.broadcasted_iota(jnp.int32, (8, 128), 0)
    piece_lane = lax.broadcasted_iota(jnp.int32, (8, 128), 1)
    lane_code = jnp.zeros((8, 128), jnp.int32)
    lane_coef = jnp.zeros((8, 128), F32)
    for comp in range(comps):
        own = lax.shift_right_logical(piece_lane, 3) == comp
        lane_code = jnp.where(own, code_of(piece_lane & 7, comp), lane_code)
        lane_coef = jnp.where(own, jnp.full((8, 128), coefs[comp].astype(F32)), lane_coef)
    for comp in range(0, comps, 2):
        block = [
            jnp.where(code_of(piece_row, here) == lane_code, lane_coef, 0.0)
            for here in (comp, comp + 1)
        ]
        match[8 * comp : 8 * comp + 16, :] = jnp.concatenate(block, axis=0).astype(BF16)

    cell_rows = lax.broadcasted_iota(jnp.int32, (GRID, 128), 0)
    lane_place = place_cell(piece_lane & (PLACES - 1))
    for part in range(GRID // 128):
        lane_cell = lane_place + jnp.where(
            piece_lane < 64, offsets[2 * part], offsets[2 * part + 1]
        )
        onehot[:, 128 * part : 128 * (part + 1)] = jnp.where(
            cell_rows == lane_cell[0:1, :], 1.0, 0.0
        ).astype(BF16)

    homeward = []
    for half in range(2):
        for copy in there[half]:
            copy.wait()
        for quarter in range(4):
            part = slice(8 * quarter, 8 * (quarter + 1))
            hi, lo = split(got[half, :, part, :].reshape(8 * comps, 128))
            both = dot(match[...], jnp.concatenate([hi, lo], axis=1))
            back[half, :, part, :] = (both[:, :128] + both[:, 128:]).reshape(comps, 8, 128)
        homeward.append(exchange(back, home, half, back_send, back_recv))

    for half in range(2):
        for copy in homeward[half]:
            copy.wait()
        hi, lo = split(home[half].reshape(GRID, 128).T)
        both = dot(jnp.concatenate([hi, lo]), h_hi)
        plain = both[:128] + both[128:] + dot(hi, h_lo)
        for pair in range(LOW // 2):
            into = slice(128 * pair, 128 * (pair + 1))
            upper, lower = plain[:64, into], plain[64:, into]
            section[block_of(2 * pair), :128] = halves(upper, swap(lower))
            section[block_of(2 * pair + 1), :128] = halves(swap(upper), lower)
        both = dot(onehot[...], jnp.concatenate(split(section[:, :128]), axis=1))
        out_ref[0, 0, :, 128 * half : 128 * (half + 1)] = both[:, :128] + both[:, 128:]


def on_device(modal_coefs, comp_levels, comp_coefs, velocity):
    comps = lax.axis_size("comp")
    shards = lax.axis_size("shard")
    stiff, lift, trace, hier = tables()
    anywhere = pl.BlockSpec(memory_space=pl.ANY)
    dma = pltpu.SemaphoreType.DMA
    exchanged = pltpu.VMEM((2, comps, GRID // comps, 128), F32)
    return pl.pallas_call(
        functools.partial(kernel, comps, shards),
        out_shape=jax.ShapeDtypeStruct(modal_coefs.shape, F32),
        in_specs=[anywhere] * 8,
        out_specs=pl.BlockSpec(memory_space=pltpu.VMEM),
        scratch_shapes=[
            pltpu.SMEM((3, comps), jnp.int32),
            pltpu.SMEM((comps,), jnp.int32),
            pltpu.SMEM((4,), F32),
            pltpu.VMEM((GRID, COEF), F32),
            pltpu.VMEM(stiff.shape, F32),
            pltpu.VMEM(lift.shape, F32),
            pltpu.VMEM(trace.shape, BF16),
            pltpu.VMEM(hier.shape, BF16),
            pltpu.VMEM((GRID, GRID), BF16),
            pltpu.VMEM((8 * comps, 8 * comps), BF16),
            pltpu.VMEM((3 * COEF, COEF), BF16),
            pltpu.VMEM((3 * COEF, COEF), BF16),
            pltpu.VMEM((GRID, COEF), F32),
            pltpu.VMEM((2 * LOW, PLACES, 128), F32),
            pltpu.VMEM((3 * LOW, PLACES, 128), F32),
            pltpu.VMEM((GRID, COEF), F32),
            pltpu.VMEM((GRID, COEF), F32),
            pltpu.VMEM((2, LOW // 2, PLACES, 128), F32),
            pltpu.VMEM((2, LOW // 2, PLACES, 128), F32),
            pltpu.VMEM((2, 2 * 128, GRID), BF16),
            exchanged,
            exchanged,
            exchanged,
            exchanged,
            dma((8,)),
            dma((2,)),
            dma((2,)),
            dma((2, comps)),
            dma((2, comps)),
            dma((2, comps)),
            dma((2, comps)),
        ],
        compiler_params=pltpu.CompilerParams(
            collective_id=0, has_side_effects=True, vmem_limit_bytes=VMEM_LIMIT
        ),
        name="combine",
    )(
        comp_levels.T,
        comp_coefs,
        velocity,
        modal_coefs,
        jnp.asarray(stiff),
        jnp.asarray(lift),
        jnp.asarray(trace),
        jnp.asarray(hier),
    )


def solution(mesh):
    placed = (P("comp", "shard", None, None), P(), P(), P())
    return jax.shard_map(
        on_device,
        mesh=mesh,
        in_specs=placed,
        out_specs=P("comp", "shard", None, None),
        check_vma=False,
    )
```

```python
import functools

import jax
import jax.numpy as jnp
import ml_dtypes
import numpy as np
from jax import lax
from jax.experimental import pallas as pl
from jax.experimental.pallas import tpu as pltpu
from jax.sharding import PartitionSpec as P

COEF = 256
BASE = 2
RISE = 3
GRID = 512
LOW = 2**RISE
PLACES = (2**BASE) ** 3
KINDS = (RISE + 1) * (RISE + 2) // 2
BF16 = jnp.bfloat16
F32 = jnp.float32
MESH = pl.DeviceIdType.MESH

courant = 0.1
VMEM_LIMIT = 62 * 2**20
ORDER = (8, 4, 12, 5, 11, 3, 13, 6, 10, 2, 14, 7, 9, 1, 15)
LEFT = [float((-1) ** order * np.sqrt((2 * order + 1) / 2.0)) for order in range(4)]
RIGHT_LEFT = float(sum((-1) ** order * (2 * order + 1) / 2.0 for order in range(4)))


def legendre(order, points):
    values = np.asarray(points) * 1.0
    if order == 0:
        poly = values * 0.0 + 1.0
    elif order == 1:
        poly = values
    elif order == 2:
        poly = (3.0 * values * values - 1.0) / 2.0
    else:
        poly = (5.0 * values * values * values - 3.0 * values) / 2.0
    return np.sqrt((2 * order + 1) / 2.0) * poly


def line_tables():
    nodes = np.array(
        [-0.8611363115940526, -0.3399810435848563, 0.3399810435848563, 0.8611363115940526]
    )
    weights = np.array(
        [0.3478548451374538, 0.6521451548625461, 0.6521451548625461, 0.3478548451374538]
    )
    stiff = np.zeros((4, 4))
    coarse = np.zeros((4, 8))
    for row in range(4):
        for column in range(4):
            if column < row and (row + column) % 2 == 1:
                stiff[row, column] = np.sqrt((2.0 * row + 1.0) * (2.0 * column + 1.0))
            coarse[row, column] = np.sum(
                weights * legendre(row, (nodes - 1.0) / 2.0) * legendre(column, nodes)
            ) / np.sqrt(2.0)
            coarse[row, column + 4] = np.sum(
                weights * legendre(row, (nodes + 1.0) / 2.0) * legendre(column, nodes)
            ) / np.sqrt(2.0)
    right = np.array([float(legendre(order, 1.0)) for order in range(4)])
    left = np.array([float(legendre(order, -1.0)) for order in range(4)])
    rows = [coarse[index] for index in range(4)]
    for index in range(4, 8):
        vector = np.eye(8)[index]
        for other in rows:
            vector = vector - np.dot(other, vector) * other
        rows.append(vector / np.sqrt(np.sum(vector * vector)))
    return (stiff - np.outer(right, right), right, left, np.array(rows))


def along(matrix, axis):
    return np.kron(np.eye(4**axis), np.kron(matrix, np.eye(4 ** (3 - axis))))


def first_basis():
    interior, _, left, _ = line_tables()
    turned, _ = np.linalg.qr(np.stack([left, interior @ left], axis=1), mode="complete")
    return np.concatenate([turned[:, 2:], turned[:, :2]], axis=1).T


def split_table(table):
    hi = table.astype(ml_dtypes.bfloat16)
    lo = (table - hi.astype(np.float64)).astype(ml_dtypes.bfloat16)
    return np.stack([hi, lo], axis=-3)


def line_hierarchy(filters, rise):
    cells = 2**rise
    whole = np.eye(cells * 4).reshape(cells, 4, cells * 4)
    for level_step in range(rise):
        for first in range(0, cells, 2 ** (level_step + 1)):
            second = first + 2**level_step
            pair = np.concatenate([whole[first], whole[second]], axis=0)
            mixed = filters @ pair
            whole[first], whole[second] = mixed[:4], mixed[4:]
    ordered = np.zeros_like(whole)
    for low in range(cells):
        digit = 0
        if low > 0:
            zeros = (low & -low).bit_length() - 1
            height = rise - zeros
            digit = 2 ** (height - 1) + (low >> (zeros + 1))
        ordered[digit] = whole[low]
    return ordered.reshape(cells, 4, cells, 4)


def compositions():
    return [(a, b, RISE - a - b) for a in range(RISE + 1) for b in range(RISE + 1 - a)]


@functools.lru_cache(None)
def tables():
    interior, right, left, filters = line_tables()
    stiff = np.stack([along(interior, axis).T for axis in range(4)]).astype(np.float32)
    lift = np.concatenate([along(left[:, None], axis).T for axis in range(4)]).astype(np.float32)
    trace = np.concatenate([along(right[None, :], axis) for axis in range(4)], axis=0).T
    lines = [line_hierarchy(filters, rise) for rise in range(RISE + 1)]
    hier = []
    for one, two, three in compositions():
        whole = np.einsum("aqlp,brms,cuno->qruabclmnpso", lines[one], lines[two], lines[three])
        hier.append(whole.reshape(GRID, GRID))
    hi, lo = split_table(trace)
    return stiff, lift, np.concatenate([hi, hi, lo]), split_table(np.stack(hier))


def split(values):
    hi = values.astype(BF16)
    return hi, (values - hi.astype(F32)).astype(BF16)


def dot(one, two):
    return jnp.dot(one, two, preferred_element_type=F32)


def dot_nt(one, two):
    return lax.dot_general(one, two, (((1,), (1,)), ((), ())), preferred_element_type=F32)


def triple(hi, lo):
    return jnp.concatenate([hi, lo, hi], axis=1)


def kernel(
    comps,
    shards,
    levels_hbm,
    coefs_hbm,
    velocity_hbm,
    x_hbm,
    stiff_hbm,
    lift_hbm,
    trace_hbm,
    hier_hbm,
    out_ref,
    levels,
    coefs,
    velocity,
    x_v,
    stiff_v,
    lift_v,
    trace_v,
    hier_v,
    onehot,
    match,
    wide,
    lifts,
    field,
    traces1,
    traces2,
    shifted,
    section,
    inside,
    edge_out,
    edge_in,
    rows,
    sent,
    got,
    back,
    home,
    local_sem,
    edge_send,
    edge_recv,
    there_send,
    there_recv,
    back_send,
    back_recv,
):
    me = lax.axis_index("comp")
    spot = lax.axis_index("shard")
    ahead = lax.rem(spot + 1, shards)
    behind = lax.rem(spot + shards - 1, shards)

    def fetch(source, target, index):
        copy = pltpu.make_async_copy(source, target, local_sem.at[index])
        copy.start()
        return copy

    levels_copy = fetch(levels_hbm, levels, 0)
    x_copy = fetch(x_hbm.at[0, 0], x_v, 1)
    velocity_copy = fetch(velocity_hbm, velocity, 2)
    trace_copy = fetch(trace_hbm, trace_v, 3)
    stiff_copy = fetch(stiff_hbm, stiff_v, 4)
    lift_copy = fetch(lift_hbm, lift_v, 5)
    coefs_copy = fetch(coefs_hbm, coefs, 6)
    hier_copy = fetch(hier_hbm, hier_v, 7)

    barrier = pltpu.get_barrier_semaphore()
    for step in range(1, comps):
        pl.semaphore_signal(
            barrier, inc=1, device_id={"comp": lax.rem(me + step, comps)}, device_id_type=MESH
        )
    pl.semaphore_signal(barrier, inc=1, device_id={"shard": ahead}, device_id_type=MESH)
    pl.semaphore_signal(barrier, inc=1, device_id={"shard": behind}, device_id_type=MESH)

    levels_copy.wait()

    def rise_of(comp, axis):
        return jnp.clip(levels[axis, comp] - BASE, 0, RISE)

    rise1 = rise_of(me, 0)
    rise2 = rise_of(me, 1)
    rise3 = rise_of(me, 2)
    kind = jnp.clip(lax.shift_right_logical(rise1 * (9 - rise1), 1) + rise2, 0, KINDS - 1)
    one = jnp.int32(1)

    def low_digits(low):
        low3 = low & (lax.shift_left(one, rise3) - 1)
        low2 = lax.shift_right_logical(low, rise3) & (lax.shift_left(one, rise2) - 1)
        low1 = lax.shift_right_logical(low, rise2 + rise3)
        return low1, low2, low3

    def cell_of(digit1, digit2, digit3):
        return (
            lax.shift_left(digit1, rise2 + rise3 + 2 * BASE)
            + lax.shift_left(digit2, rise3 + BASE)
            + digit3
        )

    offsets = [cell_of(*low_digits(jnp.int32(low))) for low in range(LOW)]

    def place_cell(place):
        return cell_of(
            lax.shift_left(lax.shift_right_logical(place, 4) & 3, jnp.full(place.shape, rise1)),
            lax.shift_left(lax.shift_right_logical(place, 2) & 3, jnp.full(place.shape, rise2)),
            lax.shift_left(place & 3, jnp.full(place.shape, rise3)),
        )

    place_row = lax.broadcasted_iota(jnp.int32, (PLACES, 128), 0)
    lanes = lax.broadcasted_iota(jnp.int32, (PLACES, 128), 1)
    left_half = lanes < 64
    place_rows = place_cell(place_row)
    for low in range(LOW):
        for part in range(GRID // 128):
            hit = (place_rows + offsets[low]) == (lanes + 128 * part)
            onehot[low * PLACES : (low + 1) * PLACES, 128 * part : 128 * (part + 1)] = jnp.where(
                hit, 1.0, 0.0
            ).astype(BF16)

    x_copy.wait()
    hi, lo = split(x_v[...])
    new_hi, new_lo = dot(onehot[...], hi), dot(onehot[...], lo)
    field[...] = new_hi + new_lo
    thrice = triple(new_hi.astype(BF16), new_lo.astype(BF16))

    def halves(one, two):
        return jnp.where(left_half, one, two)

    def swap(values):
        return pltpu.roll(values, 64, 1)

    def block_of(low):
        return slice(low * PLACES, (low + 1) * PLACES)

    def pack(values, low):
        return halves(values[block_of(low), :], swap(values[block_of(low + LOW // 2), :]))

    def send_edge(stage):
        copy = pltpu.make_async_remote_copy(
            src_ref=edge_out.at[stage],
            dst_ref=edge_in.at[stage],
            send_sem=edge_send.at[stage],
            recv_sem=edge_recv.at[stage],
            device_id={"shard": ahead},
            device_id_type=MESH,
        )
        copy.start()
        return copy

    trace_copy.wait()
    trace = dot(thrice, trace_v[...])
    for low in range(LOW // 2):
        edge_out[0, low] = pack(trace[:, :128], low)
    pl.semaphore_wait(barrier, comps + 1)
    edge_copy = send_edge(0)

    velocity_copy.wait()
    reach = None
    for comp in range(comps):
        total = velocity[0] * (1.0 * shards)
        for axis in range(3):
            size = lax.shift_left(one, levels[axis, comp]).astype(F32)
            total = total + velocity[axis + 1] * size
        reach = total if reach is None else jnp.maximum(reach, total)
    step_size = jnp.full((1, COEF), courant, F32) / jnp.full((1, COEF), reach, F32)
    sizes = [jnp.float32(shards)] + [
        lax.shift_left(one, levels[axis, me]).astype(F32) for axis in range(3)
    ]
    scales = [step_size * (2.0 * velocity[axis] * sizes[axis]) for axis in range(4)]
    stiff_copy.wait()
    volume = scales[0] * stiff_v[0]
    for axis in range(1, 4):
        volume = volume + scales[axis] * stiff_v[axis]
    hi, lo = split(volume)
    wide[:COEF], wide[COEF : 2 * COEF], wide[2 * COEF :] = hi, hi, lo
    lift_copy.wait()
    for part in range(3):
        lifts[part * COEF : part * COEF + 64, :] = jnp.zeros((64, COEF), BF16)
    for axis in range(1, 4):
        hi, lo = split(scales[axis] * lift_v[64 * axis : 64 * (axis + 1), :])
        for part, piece in enumerate((hi, hi, lo)):
            start = part * COEF + 64 * axis
            lifts[start : start + 64, :] = piece
    lift_first = [
        scales[0][:, :128] * jnp.where(left_half[:1], LEFT[2 * group], LEFT[2 * group + 1])
        for group in range(2)
    ]
    edge_factor = scales[0][:, :128] * RIGHT_LEFT

    def behind_of(low, axis):
        digits = list(low_digits(jnp.int32(low)))
        rise = (rise1, rise2, rise3)[axis]
        first = digits[axis] == 0
        digits[axis] = (digits[axis] + lax.shift_left(one, rise) - 1) & (
            lax.shift_left(one, rise) - 1
        )
        spot = (
            lax.shift_left(digits[0], rise2 + rise3) + lax.shift_left(digits[1], rise3) + digits[2]
        )
        return spot & (LOW - 1), first

    sources = []
    for low in range(LOW):
        spot1, first1 = behind_of(low, 0)
        spot2, first2 = behind_of(low, 1)
        spot3, first3 = behind_of(low, 2)
        sources.append(
            (
                spot1 + jnp.where(first1, LOW, 0),
                spot2 + jnp.where(first2, LOW, 0),
                spot3 + jnp.where(first3, 2 * LOW, 0),
            )
        )

    def inner_slope(thrice, trace):
        for low in range(LOW):
            now = trace[block_of(low), :128]
            traces1[low] = now
            traces1[LOW + low] = pltpu.roll(now, 16, 0)
            now = trace[block_of(low), 128:]
            traces2[low] = now
            traces2[LOW + low] = jnp.where(
                (place_row & 15) < 4, pltpu.roll(now, PLACES - 12, 0), pltpu.roll(now, 4, 0)
            )
            traces2[2 * LOW + low] = jnp.where(
                (place_row & 3) < 1, pltpu.roll(now, PLACES - 3, 0), pltpu.roll(now, 1, 0)
            )
        inner = dot(thrice, wide[...])
        for low in range(LOW):
            from1, from2, from3 = sources[low]
            shifted[block_of(low), :128] = traces1[from1]
            shifted[block_of(low), 128:] = halves(traces2[from2], traces2[from3])
        return inner + dot(triple(*split(shifted[...])), lifts[...])

    def add_edge(stage, factor):
        for low in range(LOW // 2):
            edge = edge_in[stage, low]
            turned = swap(edge)
            for place, both in (
                (low, halves(edge, turned)),
                (low + LOW // 2, halves(turned, edge)),
            ):
                for group in range(2):
                    columns = slice(128 * group, 128 * (group + 1))
                    section[block_of(place), columns] += (factor * lift_first[group]) * both

    def advance(trace, thrice):
        return 0.5 * field[...] + 0.5 * (section[...] + inner_slope(thrice, trace))

    basis = first_basis()

    def exchange(source, target, half, send_sem, recv_sem):
        copies = []
        for step in ORDER:
            other = lax.rem(me + step, comps)
            copy = pltpu.make_async_remote_copy(
                src_ref=source.at[half, other],
                dst_ref=target.at[half, me],
                send_sem=send_sem.at[half, step],
                recv_sem=recv_sem.at[half, step],
                device_id={"comp": other},
                device_id_type=MESH,
            )
            copy.start()
            copies.append(copy)
        target[half, me] = source[half, me]
        return copies

    def to_owners(half):
        for pair in range(LOW // 2):
            blocks = []
            for group in range(2):
                columns = slice(128 * group, 128 * (group + 1))
                even = section[block_of(2 * pair), columns]
                odd = section[block_of(2 * pair + 1), columns]
                blocks += [halves(even, swap(odd)), halves(swap(even), odd)]
            turned = [
                sum(float(basis[row, first]) * blocks[first] for first in range(4))
                for row in (2 * half, 2 * half + 1)
            ]
            into = slice(128 * pair, 128 * (pair + 1))
            hi, lo = split(jnp.concatenate(turned))
            rows[half, :128, into] = hi
            rows[half, 128:, into] = lo
        both = dot_nt(h_hi, rows[half])
        whole = both[:, :128] + both[:, 128:] + dot_nt(h_lo, rows[half, :128])
        sent[half] = whole.reshape(sent.shape[1:])
        return exchange(sent, got, half, there_send, there_recv)

    section[...] = field[...] + inner_slope(thrice, trace)
    inside[...] = section[...]
    thrice = triple(*split(section[...]))
    trace = dot(thrice, trace_v[...])
    for low in range(LOW // 2):
        edge_out[1, low] = pack(trace[:, :128], low)
    section[...] = advance(trace, thrice)
    edge_copy.wait()
    for low in range(LOW // 2):
        edge_out[1, low] += edge_factor * edge_in[0, low]
    edge_copy = send_edge(1)
    hier_copy.wait()
    h_hi, h_lo = hier_v[kind, 0], hier_v[kind, 1]
    there = [to_owners(0)]

    section[...] = inside[...]
    add_edge(0, 1.0)
    thrice = triple(*split(section[...]))
    section[...] = advance(dot(thrice, trace_v[...]), thrice)
    edge_copy.wait()
    add_edge(1, 0.5)
    there.append(to_owners(1))

    coefs_copy.wait()

    def code_of(digits, comp):
        up2 = rise_of(comp, 1)
        up3 = rise_of(comp, 2)
        digit3 = digits & (lax.shift_left(one, up3) - 1)
        digit2 = lax.shift_right_logical(digits, jnp.full(digits.shape, up3)) & (
            lax.shift_left(one, up2) - 1
        )
        digit1 = lax.shift_right_logical(digits, jnp.full(digits.shape, up2 + up3))
        return digit1 * 64 + digit2 * 8 + digit3

    piece_row = lax.broadcasted_iota(jnp.int32, (8, 128), 0)
    piece_lane = lax.broadcasted_iota(jnp.int32, (8, 128), 1)
    lane_code = jnp.zeros((8, 128), jnp.int32)
    lane_coef = jnp.zeros((8, 128), F32)
    for comp in range(comps):
        own = lax.shift_right_logical(piece_lane, 3) == comp
        lane_code = jnp.where(own, code_of(piece_lane & 7, comp), lane_code)
        lane_coef = jnp.where(own, jnp.full((8, 128), coefs[comp].astype(F32)), lane_coef)
    for comp in range(0, comps, 2):
        block = [
            jnp.where(code_of(piece_row, here) == lane_code, lane_coef, 0.0)
            for here in (comp, comp + 1)
        ]
        match[8 * comp : 8 * comp + 16, :] = jnp.concatenate(block, axis=0).astype(BF16)

    cell_rows = lax.broadcasted_iota(jnp.int32, (GRID, 128), 0)
    lane_place = place_cell(piece_lane & (PLACES - 1))
    for part in range(GRID // 128):
        lane_cell = lane_place + jnp.where(
            piece_lane < 64, offsets[2 * part], offsets[2 * part + 1]
        )
        onehot[:, 128 * part : 128 * (part + 1)] = jnp.where(
            cell_rows == lane_cell[0:1, :], 1.0, 0.0
        ).astype(BF16)

    homeward = []
    for half in range(2):
        for copy in there[half]:
            copy.wait()
        for quarter in range(4):
            part = slice(8 * quarter, 8 * (quarter + 1))
            hi, lo = split(got[half, :, part, :].reshape(8 * comps, 128))
            both = dot(match[...], jnp.concatenate([hi, lo], axis=1))
            back[half, :, part, :] = (both[:, :128] + both[:, 128:]).reshape(comps, 8, 128)
        homeward.append(exchange(back, home, half, back_send, back_recv))

    for half in range(2):
        for copy in homeward[half]:
            copy.wait()
        hi, lo = split(home[half].reshape(GRID, 128).T)
        both = dot(jnp.concatenate([hi, lo]), h_hi)
        plain = both[:128] + both[128:] + dot(hi, h_lo)
        for pair in range(LOW // 2):
            into = slice(128 * pair, 128 * (pair + 1))
            upper, lower = plain[:64, into], plain[64:, into]
            section[block_of(2 * pair), :128] = halves(upper, swap(lower))
            section[block_of(2 * pair + 1), :128] = halves(swap(upper), lower)
        both = dot(onehot[...], jnp.concatenate(split(section[:, :128]), axis=1))
        turned = both[:, :128] + both[:, 128:]
        swapped = swap(turned)
        for group in range(2):
            near = [float(basis[2 * half + k, 2 * group + k]) for k in range(2)]
            far = [float(basis[2 * half + 1 - k, 2 * group + k]) for k in range(2)]
            part = (
                jnp.where(left_half[:1], near[0], near[1]) * turned
                + jnp.where(left_half[:1], far[0], far[1]) * swapped
            )
            columns = slice(128 * group, 128 * (group + 1))
            if half == 0:
                out_ref[0, 0, :, columns] = part
            else:
                out_ref[0, 0, :, columns] += part


def on_device(modal_coefs, comp_levels, comp_coefs, velocity):
    comps = lax.axis_size("comp")
    shards = lax.axis_size("shard")
    stiff, lift, trace, hier = tables()
    anywhere = pl.BlockSpec(memory_space=pl.ANY)
    dma = pltpu.SemaphoreType.DMA
    exchanged = pltpu.VMEM((2, comps, GRID // comps, 128), F32)
    return pl.pallas_call(
        functools.partial(kernel, comps, shards),
        out_shape=jax.ShapeDtypeStruct(modal_coefs.shape, F32),
        in_specs=[anywhere] * 8,
        out_specs=pl.BlockSpec(memory_space=pltpu.VMEM),
        scratch_shapes=[
            pltpu.SMEM((3, comps), jnp.int32),
            pltpu.SMEM((comps,), jnp.int32),
            pltpu.SMEM((4,), F32),
            pltpu.VMEM((GRID, COEF), F32),
            pltpu.VMEM(stiff.shape, F32),
            pltpu.VMEM(lift.shape, F32),
            pltpu.VMEM(trace.shape, BF16),
            pltpu.VMEM(hier.shape, BF16),
            pltpu.VMEM((GRID, GRID), BF16),
            pltpu.VMEM((8 * comps, 8 * comps), BF16),
            pltpu.VMEM((3 * COEF, COEF), BF16),
            pltpu.VMEM((3 * COEF, COEF), BF16),
            pltpu.VMEM((GRID, COEF), F32),
            pltpu.VMEM((2 * LOW, PLACES, 128), F32),
            pltpu.VMEM((3 * LOW, PLACES, 128), F32),
            pltpu.VMEM((GRID, COEF), F32),
            pltpu.VMEM((GRID, COEF), F32),
            pltpu.VMEM((GRID, COEF), F32),
            pltpu.VMEM((2, LOW // 2, PLACES, 128), F32),
            pltpu.VMEM((2, LOW // 2, PLACES, 128), F32),
            pltpu.VMEM((2, 2 * 128, GRID), BF16),
            exchanged,
            exchanged,
            exchanged,
            exchanged,
            dma((8,)),
            dma((2,)),
            dma((2,)),
            dma((2, comps)),
            dma((2, comps)),
            dma((2, comps)),
            dma((2, comps)),
        ],
        compiler_params=pltpu.CompilerParams(
            collective_id=0, has_side_effects=True, vmem_limit_bytes=VMEM_LIMIT
        ),
        name="combine",
    )(
        comp_levels.T,
        comp_coefs,
        velocity,
        modal_coefs,
        jnp.asarray(stiff),
        jnp.asarray(lift),
        jnp.asarray(trace),
        jnp.asarray(hier),
    )


def solution(mesh):
    placed = (P("comp", "shard", None, None), P(), P(), P())
    return jax.shard_map(
        on_device,
        mesh=mesh,
        in_specs=placed,
        out_specs=P("comp", "shard", None, None),
        check_vma=False,
    )
```

```python
import functools

import jax
import jax.numpy as jnp
import ml_dtypes
import numpy as np
from jax import lax
from jax.experimental import pallas as pl
from jax.experimental.pallas import tpu as pltpu
from jax.sharding import PartitionSpec as P

COEF = 256
BASE = 2
RISE = 3
GRID = 512
LOW = 2**RISE
PLACES = (2**BASE) ** 3
KINDS = (RISE + 1) * (RISE + 2) // 2
BF16 = jnp.bfloat16
F32 = jnp.float32
MESH = pl.DeviceIdType.MESH

courant = 0.1
VMEM_LIMIT = 62 * 2**20
ORDER = (8, 4, 12, 5, 11, 3, 13, 6, 10, 2, 14, 7, 9, 1, 15)
RIGHT_LEFT = float(sum((-1) ** order * (2 * order + 1) / 2.0 for order in range(4)))


def legendre(order, points):
    values = np.asarray(points) * 1.0
    if order == 0:
        poly = values * 0.0 + 1.0
    elif order == 1:
        poly = values
    elif order == 2:
        poly = (3.0 * values * values - 1.0) / 2.0
    else:
        poly = (5.0 * values * values * values - 3.0 * values) / 2.0
    return np.sqrt((2 * order + 1) / 2.0) * poly


def line_tables():
    nodes = np.array(
        [-0.8611363115940526, -0.3399810435848563, 0.3399810435848563, 0.8611363115940526]
    )
    weights = np.array(
        [0.3478548451374538, 0.6521451548625461, 0.6521451548625461, 0.3478548451374538]
    )
    stiff = np.zeros((4, 4))
    coarse = np.zeros((4, 8))
    for row in range(4):
        for column in range(4):
            if column < row and (row + column) % 2 == 1:
                stiff[row, column] = np.sqrt((2.0 * row + 1.0) * (2.0 * column + 1.0))
            coarse[row, column] = np.sum(
                weights * legendre(row, (nodes - 1.0) / 2.0) * legendre(column, nodes)
            ) / np.sqrt(2.0)
            coarse[row, column + 4] = np.sum(
                weights * legendre(row, (nodes + 1.0) / 2.0) * legendre(column, nodes)
            ) / np.sqrt(2.0)
    right = np.array([float(legendre(order, 1.0)) for order in range(4)])
    left = np.array([float(legendre(order, -1.0)) for order in range(4)])
    rows = [coarse[index] for index in range(4)]
    for index in range(4, 8):
        vector = np.eye(8)[index]
        for other in rows:
            vector = vector - np.dot(other, vector) * other
        rows.append(vector / np.sqrt(np.sum(vector * vector)))
    return (stiff - np.outer(right, right), right, left, np.array(rows))


def along(matrix, axis):
    return np.kron(np.eye(4**axis), np.kron(matrix, np.eye(4 ** (2 - axis))))


def twice(matrix):
    return np.kron(np.eye(2), matrix)


def first_basis():
    interior, _, left, _ = line_tables()
    turned, _ = np.linalg.qr(np.stack([left, interior @ left], axis=1), mode="complete")
    return np.concatenate([turned[:, 2:], turned[:, :2]], axis=1).T


def split_table(table):
    hi = table.astype(ml_dtypes.bfloat16)
    lo = (table - hi.astype(np.float64)).astype(ml_dtypes.bfloat16)
    return np.stack([hi, lo], axis=-3)


def line_hierarchy(filters, rise):
    cells = 2**rise
    whole = np.eye(cells * 4).reshape(cells, 4, cells * 4)
    for level_step in range(rise):
        for first in range(0, cells, 2 ** (level_step + 1)):
            second = first + 2**level_step
            pair = np.concatenate([whole[first], whole[second]], axis=0)
            mixed = filters @ pair
            whole[first], whole[second] = mixed[:4], mixed[4:]
    ordered = np.zeros_like(whole)
    for low in range(cells):
        digit = 0
        if low > 0:
            zeros = (low & -low).bit_length() - 1
            height = rise - zeros
            digit = 2 ** (height - 1) + (low >> (zeros + 1))
        ordered[digit] = whole[low]
    return ordered.reshape(cells, 4, cells, 4)


def compositions():
    return [(a, b, RISE - a - b) for a in range(RISE + 1) for b in range(RISE + 1 - a)]


@functools.lru_cache(None)
def tables():
    interior, right, left, filters = line_tables()
    stiff = np.stack([twice(along(interior, axis).T) for axis in range(3)]).astype(np.float32)
    lift = np.zeros((128, 128), np.float32)
    trace = np.zeros((128, 128))
    for axis in range(3):
        lift[32 * axis : 32 * (axis + 1)] = twice(along(left[:, None], axis).T)
        trace[:, 32 * axis : 32 * (axis + 1)] = twice(along(right[None, :], axis).T)
    lines = [line_hierarchy(filters, rise) for rise in range(RISE + 1)]
    hier = []
    for one, two, three in compositions():
        whole = np.einsum("aqlp,brms,cuno->qruabclmnpso", lines[one], lines[two], lines[three])
        hier.append(whole.reshape(GRID, GRID))
    hi, lo = split_table(trace)
    trace = np.block([[hi, lo], [hi, np.zeros_like(lo)]])
    return stiff, lift, trace, split_table(np.stack(hier))


def split(values):
    hi = values.astype(BF16)
    return hi, (values - hi.astype(F32)).astype(BF16)


def dot(one, two):
    return jnp.dot(one, two, preferred_element_type=F32)


def dot_nt(one, two):
    return lax.dot_general(one, two, (((1,), (1,)), ((), ())), preferred_element_type=F32)


def fold(values):
    return values[:, :128] + values[:, 128:]


def square(matrix):
    hi, lo = split(matrix)
    zero = jnp.zeros_like(lo)
    return jnp.concatenate(
        [jnp.concatenate([hi, lo], axis=1), jnp.concatenate([hi, zero], axis=1)], axis=0
    )


def kernel(
    comps,
    shards,
    levels_hbm,
    coefs_hbm,
    velocity_hbm,
    x_hbm,
    stiff_hbm,
    lift_hbm,
    trace_hbm,
    hier_hbm,
    out_ref,
    levels,
    coefs,
    velocity,
    x_v,
    stiff_v,
    lift_v,
    trace_v,
    hier_v,
    onehot,
    match,
    wide,
    lifts,
    field,
    other,
    traces,
    shifted,
    plane,
    edge_out,
    edge_in,
    rows,
    sent,
    got,
    back,
    home,
    local_sem,
    edge_send,
    edge_recv,
    there_send,
    there_recv,
    back_send,
    back_recv,
):
    me = lax.axis_index("comp")
    spot = lax.axis_index("shard")
    ahead = lax.rem(spot + 1, shards)
    behind = lax.rem(spot + shards - 1, shards)

    def fetch(source, target, index):
        copy = pltpu.make_async_copy(source, target, local_sem.at[index])
        copy.start()
        return copy

    levels_copy = fetch(levels_hbm, levels, 0)
    x_copy = fetch(x_hbm.at[0, 0], x_v, 1)
    velocity_copy = fetch(velocity_hbm, velocity, 2)
    trace_copy = fetch(trace_hbm, trace_v, 3)
    stiff_copy = fetch(stiff_hbm, stiff_v, 4)
    lift_copy = fetch(lift_hbm, lift_v, 5)
    coefs_copy = fetch(coefs_hbm, coefs, 6)
    hier_copy = fetch(hier_hbm, hier_v, 7)

    barrier = pltpu.get_barrier_semaphore()
    for step in range(1, comps):
        pl.semaphore_signal(
            barrier, inc=1, device_id={"comp": lax.rem(me + step, comps)}, device_id_type=MESH
        )
    pl.semaphore_signal(barrier, inc=1, device_id={"shard": ahead}, device_id_type=MESH)
    pl.semaphore_signal(barrier, inc=1, device_id={"shard": behind}, device_id_type=MESH)

    levels_copy.wait()

    def rise_of(comp, axis):
        return jnp.clip(levels[axis, comp] - BASE, 0, RISE)

    rise1 = rise_of(me, 0)
    rise2 = rise_of(me, 1)
    rise3 = rise_of(me, 2)
    kind = jnp.clip(lax.shift_right_logical(rise1 * (9 - rise1), 1) + rise2, 0, KINDS - 1)
    one = jnp.int32(1)

    def low_digits(low):
        low3 = low & (lax.shift_left(one, rise3) - 1)
        low2 = lax.shift_right_logical(low, rise3) & (lax.shift_left(one, rise2) - 1)
        low1 = lax.shift_right_logical(low, rise2 + rise3)
        return low1, low2, low3

    def cell_of(digit1, digit2, digit3):
        return (
            lax.shift_left(digit1, rise2 + rise3 + 2 * BASE)
            + lax.shift_left(digit2, rise3 + BASE)
            + digit3
        )

    offsets = [cell_of(*low_digits(jnp.int32(low))) for low in range(LOW)]

    def place_cell(place):
        return cell_of(
            lax.shift_left(lax.shift_right_logical(place, 4) & 3, jnp.full(place.shape, rise1)),
            lax.shift_left(lax.shift_right_logical(place, 2) & 3, jnp.full(place.shape, rise2)),
            lax.shift_left(place & 3, jnp.full(place.shape, rise3)),
        )

    place_row = lax.broadcasted_iota(jnp.int32, (PLACES, 128), 0)
    lanes = lax.broadcasted_iota(jnp.int32, (PLACES, 128), 1)
    left_half = lanes < 64
    place_rows = place_cell(place_row)
    for low in range(LOW):
        for part in range(GRID // 128):
            hit = (place_rows + offsets[low]) == (lanes + 128 * part)
            onehot[low * PLACES : (low + 1) * PLACES, 128 * part : 128 * (part + 1)] = jnp.where(
                hit, 1.0, 0.0
            ).astype(BF16)

    def halves(one, two):
        return jnp.where(left_half, one, two)

    def swap(values):
        return pltpu.roll(values, 64, 1)

    def block_of(low):
        return slice(low * PLACES, (low + 1) * PLACES)

    def blocks(values):
        return [values[block_of(low), :] for low in range(LOW)]

    x_copy.wait()
    hi, lo = split(x_v[...])
    now = dot(onehot[...], hi) + dot(onehot[...], lo)
    field[...] = now
    other[:, :128] = swap(now[:, :128])
    other[:, 128:] = swap(now[:, 128:])

    basis = first_basis()
    interior, right, left, _ = line_tables()

    def pair_of(rows_of):
        return [
            jnp.where(left_half[:1], float(rows_of[0][first]), float(rows_of[1][second]))
            for first, second in ((0, 1), (1, 0), (2, 3), (3, 2))
        ]

    def mix(factors):
        return (
            factors[0] * field[:, :128]
            + factors[1] * other[:, :128]
            + factors[2] * field[:, 128:]
            + factors[3] * other[:, 128:]
        )

    def edge_copy(stage):
        return pltpu.make_async_remote_copy(
            src_ref=edge_out.at[stage],
            dst_ref=edge_in.at[stage],
            send_sem=edge_send.at[stage],
            recv_sem=edge_recv.at[stage],
            device_id={"shard": ahead},
            device_id_type=MESH,
        )

    def pack(stage, values):
        parts = blocks(values)
        for low in range(LOW // 2):
            edge_out[stage, low] = halves(parts[low], parts[low + LOW // 2])

    pack(0, mix(pair_of([right, right])))
    pl.semaphore_wait(barrier, comps + 1)
    first_edge, second_edge = edge_copy(0), edge_copy(1)
    first_edge.start()

    velocity_copy.wait()
    reach = None
    for comp in range(comps):
        total = velocity[0] * (1.0 * shards)
        for axis in range(3):
            size = lax.shift_left(one, levels[axis, comp]).astype(F32)
            total = total + velocity[axis + 1] * size
        reach = total if reach is None else jnp.maximum(reach, total)
    step_size = jnp.full((1, 128), courant, F32) / jnp.full((1, 128), reach, F32)
    sizes = [jnp.float32(shards)] + [
        lax.shift_left(one, levels[axis, me]).astype(F32) for axis in range(3)
    ]
    first_scale, *scales = [
        step_size * (2.0 * velocity[axis] * sizes[axis]) for axis in range(4)
    ]
    stiff_copy.wait()
    wide[...] = square(
        scales[0] * stiff_v[0] + scales[1] * stiff_v[1] + scales[2] * stiff_v[2]
    )
    lift_copy.wait()
    scale_rows = [jnp.broadcast_to(scale, (32, 128)) for scale in scales]
    lifts[...] = square(
        jnp.concatenate([*scale_rows, jnp.zeros((32, 128), F32)], axis=0) * lift_v[...]
    )

    def behind_of(low, axis):
        digits = list(low_digits(jnp.int32(low)))
        rise = (rise1, rise2, rise3)[axis]
        first = digits[axis] == 0
        digits[axis] = (digits[axis] + lax.shift_left(one, rise) - 1) & (
            lax.shift_left(one, rise) - 1
        )
        spot = (
            lax.shift_left(digits[0], rise2 + rise3) + lax.shift_left(digits[1], rise3) + digits[2]
        )
        return (spot & (LOW - 1)) + jnp.where(first, LOW, 0)

    sources = [[behind_of(low, axis) for axis in range(3)] for low in range(LOW)]

    def by_axis(one, two, three):
        return jnp.where(lanes < 32, one, jnp.where(lanes < 64, two, three))

    def others_step(values):
        pair = jnp.concatenate(split(values), axis=1)
        for low, now in enumerate(blocks(fold(dot(pair, trace_v[...])))):
            traces[low] = now
            traces[LOW + low] = by_axis(
                pltpu.roll(now, 16, 0),
                jnp.where(
                    (place_row & 15) < 4, pltpu.roll(now, PLACES - 12, 0), pltpu.roll(now, 4, 0)
                ),
                jnp.where(
                    (place_row & 3) < 1, pltpu.roll(now, PLACES - 3, 0), pltpu.roll(now, 1, 0)
                ),
            )
        inner = dot(pair, wide[...])
        for low in range(LOW):
            shifted[block_of(low), :] = by_axis(*[traces[source] for source in sources[low]])
        return fold(inner + dot(jnp.concatenate(split(shifted[...]), axis=1), lifts[...]))

    def combinations(half):
        plain, once, square_of = [
            pair_of(matrix[2 * half : 2 * half + 2])
            for matrix in (basis, basis @ interior, basis @ interior @ interior)
        ]
        step = first_scale
        return (
            mix(plain),
            mix([2.0 * (p + step * o) for p, o in zip(plain, once)]),
            mix([p + step * (o + 0.5 * step * q) for p, o, q in zip(plain, once, square_of)]),
        )

    def edge_at(stage, low):
        edge = edge_in[stage, low % (LOW // 2)]
        turned = swap(edge)
        return halves(edge, turned) if low < LOW // 2 else halves(turned, edge)

    pack(1, mix([first_scale * part for part in pair_of([right @ interior] * 2)]))

    def exchange(source, target, half, send_sem, recv_sem):
        copies = []
        for step in ORDER:
            other = lax.rem(me + step, comps)
            copy = pltpu.make_async_remote_copy(
                src_ref=source.at[half, other],
                dst_ref=target.at[half, me],
                send_sem=send_sem.at[half, step],
                recv_sem=recv_sem.at[half, step],
                device_id={"comp": other},
                device_id_type=MESH,
            )
            copy.start()
            copies.append(copy)
        target[half, me] = source[half, me]
        return copies

    def to_owners(half, advanced):
        parts = blocks(advanced)
        for pair in range(LOW // 2):
            even, odd = parts[2 * pair], parts[2 * pair + 1]
            into = slice(128 * pair, 128 * (pair + 1))
            hi, lo = split(jnp.concatenate([halves(even, swap(odd)), halves(swap(even), odd)]))
            rows[half, :128, into] = hi
            rows[half, 128:, into] = lo
        both = dot_nt(h_hi, rows[half])
        whole = fold(both) + dot_nt(h_lo, rows[half, :128])
        sent[half] = whole.reshape(sent.shape[1:])
        return exchange(sent, got, half, there_send, there_recv)

    def pass_edge():
        first_edge.wait()
        for low in range(LOW // 2):
            edge_out[1, low] += (first_scale * RIGHT_LEFT) * edge_in[0, low]
        second_edge.start()

    trace_copy.wait()
    y, m, u = combinations(0)
    advanced = u + 0.5 * others_step(m + others_step(y))
    hier_copy.wait()
    h_hi, h_lo = hier_v[kind, 0], hier_v[kind, 1]
    there = [to_owners(0, advanced)]

    pass_edge()
    y, m, u = combinations(1)
    bent = basis @ interior @ left
    straight = float(basis[2] @ left)
    to_m = jnp.where(left_half[:1], 2.0 * straight * first_scale, 0.0)
    to_u = first_scale * jnp.where(
        left_half[:1],
        straight + 0.5 * float(bent[2]) * first_scale,
        0.5 * float(bent[3]) * first_scale,
    )
    to_u2 = jnp.where(left_half[:1], 0.5 * straight * first_scale, 0.0)
    edges = jnp.concatenate([edge_at(0, low) for low in range(LOW)], axis=0)
    plane[...] = u + to_u * edges + 0.5 * others_step(m + to_m * edges + others_step(y))
    second_edge.wait()
    edges = jnp.concatenate([edge_at(1, low) for low in range(LOW)], axis=0)
    there.append(to_owners(1, plane[...] + to_u2 * edges))

    coefs_copy.wait()

    def code_of(digits, comp):
        up2 = rise_of(comp, 1)
        up3 = rise_of(comp, 2)
        digit3 = digits & (lax.shift_left(one, up3) - 1)
        digit2 = lax.shift_right_logical(digits, jnp.full(digits.shape, up3)) & (
            lax.shift_left(one, up2) - 1
        )
        digit1 = lax.shift_right_logical(digits, jnp.full(digits.shape, up2 + up3))
        return digit1 * 64 + digit2 * 8 + digit3

    piece_row = lax.broadcasted_iota(jnp.int32, (8, 128), 0)
    piece_lane = lax.broadcasted_iota(jnp.int32, (8, 128), 1)
    lane_code = jnp.zeros((8, 128), jnp.int32)
    lane_coef = jnp.zeros((8, 128), F32)
    for comp in range(comps):
        own = lax.shift_right_logical(piece_lane, 3) == comp
        lane_code = jnp.where(own, code_of(piece_lane & 7, comp), lane_code)
        lane_coef = jnp.where(own, jnp.full((8, 128), coefs[comp].astype(F32)), lane_coef)
    for comp in range(0, comps, 2):
        block = [
            jnp.where(code_of(piece_row, here) == lane_code, lane_coef, 0.0)
            for here in (comp, comp + 1)
        ]
        match[8 * comp : 8 * comp + 16, :] = jnp.concatenate(block, axis=0).astype(BF16)

    cell_rows = lax.broadcasted_iota(jnp.int32, (GRID, 128), 0)
    lane_place = place_cell(piece_lane & (PLACES - 1))
    for part in range(GRID // 128):
        lane_cell = lane_place + jnp.where(
            piece_lane < 64, offsets[2 * part], offsets[2 * part + 1]
        )
        onehot[:, 128 * part : 128 * (part + 1)] = jnp.where(
            cell_rows == lane_cell[0:1, :], 1.0, 0.0
        ).astype(BF16)

    homeward = []
    for half in range(2):
        for copy in there[half]:
            copy.wait()
        for quarter in range(4):
            part = slice(8 * quarter, 8 * (quarter + 1))
            hi, lo = split(got[half, :, part, :].reshape(8 * comps, 128))
            both = dot(match[...], jnp.concatenate([hi, lo], axis=1))
            back[half, :, part, :] = fold(both).reshape(comps, 8, 128)
        homeward.append(exchange(back, home, half, back_send, back_recv))

    for half in range(2):
        for copy in homeward[half]:
            copy.wait()
        hi, lo = split(home[half].reshape(GRID, 128).T)
        both = dot(jnp.concatenate([hi, lo]), h_hi)
        plain = both[:128] + both[128:] + dot(hi, h_lo)
        for pair in range(LOW // 2):
            into = slice(128 * pair, 128 * (pair + 1))
            upper, lower = plain[:64, into], plain[64:, into]
            plane[block_of(2 * pair), :] = halves(upper, swap(lower))
            plane[block_of(2 * pair + 1), :] = halves(swap(upper), lower)
        turned = fold(dot(onehot[...], jnp.concatenate(split(plane[...]), axis=1)))
        swapped = swap(turned)
        for group in range(2):
            near = [float(basis[2 * half + k, 2 * group + k]) for k in range(2)]
            far = [float(basis[2 * half + 1 - k, 2 * group + k]) for k in range(2)]
            part = (
                jnp.where(left_half[:1], near[0], near[1]) * turned
                + jnp.where(left_half[:1], far[0], far[1]) * swapped
            )
            columns = slice(128 * group, 128 * (group + 1))
            if half == 0:
                out_ref[0, 0, :, columns] = part
            else:
                out_ref[0, 0, :, columns] += part


def on_device(modal_coefs, comp_levels, comp_coefs, velocity):
    comps = lax.axis_size("comp")
    shards = lax.axis_size("shard")
    stiff, lift, trace, hier = tables()
    anywhere = pl.BlockSpec(memory_space=pl.ANY)
    dma = pltpu.SemaphoreType.DMA
    exchanged = pltpu.VMEM((2, comps, GRID // comps, 128), F32)
    return pl.pallas_call(
        functools.partial(kernel, comps, shards),
        out_shape=jax.ShapeDtypeStruct(modal_coefs.shape, F32),
        in_specs=[anywhere] * 8,
        out_specs=pl.BlockSpec(memory_space=pltpu.VMEM),
        scratch_shapes=[
            pltpu.SMEM((3, comps), jnp.int32),
            pltpu.SMEM((comps,), jnp.int32),
            pltpu.SMEM((4,), F32),
            pltpu.VMEM((GRID, COEF), F32),
            pltpu.VMEM(stiff.shape, F32),
            pltpu.VMEM(lift.shape, F32),
            pltpu.VMEM(trace.shape, BF16),
            pltpu.VMEM(hier.shape, BF16),
            pltpu.VMEM((GRID, GRID), BF16),
            pltpu.VMEM((8 * comps, 8 * comps), BF16),
            pltpu.VMEM((COEF, COEF), BF16),
            pltpu.VMEM((COEF, COEF), BF16),
            pltpu.VMEM((GRID, COEF), F32),
            pltpu.VMEM((GRID, COEF), F32),
            pltpu.VMEM((2 * LOW, PLACES, 128), F32),
            pltpu.VMEM((GRID, 128), F32),
            pltpu.VMEM((GRID, 128), F32),
            pltpu.VMEM((2, LOW // 2, PLACES, 128), F32),
            pltpu.VMEM((2, LOW // 2, PLACES, 128), F32),
            pltpu.VMEM((2, 2 * 128, GRID), BF16),
            exchanged,
            exchanged,
            exchanged,
            exchanged,
            dma((8,)),
            dma((2,)),
            dma((2,)),
            dma((2, comps)),
            dma((2, comps)),
            dma((2, comps)),
            dma((2, comps)),
        ],
        compiler_params=pltpu.CompilerParams(
            collective_id=0, has_side_effects=True, vmem_limit_bytes=VMEM_LIMIT
        ),
        name="combine",
    )(
        comp_levels.T,
        comp_coefs,
        velocity,
        modal_coefs,
        jnp.asarray(stiff),
        jnp.asarray(lift),
        jnp.asarray(trace),
        jnp.asarray(hier),
    )


def solution(mesh):
    placed = (P("comp", "shard", None, None), P(), P(), P())
    return jax.shard_map(
        on_device,
        mesh=mesh,
        in_specs=placed,
        out_specs=P("comp", "shard", None, None),
        check_vma=False,
    )
```

```python
import functools

import jax
import jax.numpy as jnp
import ml_dtypes
import numpy as np
from jax import lax
from jax.experimental import pallas as pl
from jax.experimental.pallas import tpu as pltpu
from jax.sharding import PartitionSpec as P

COEF = 256
BASE = 2
RISE = 3
GRID = 512
LOW = 2**RISE
PLACES = (2**BASE) ** 3
KINDS = (RISE + 1) * (RISE + 2) // 2
BF16 = jnp.bfloat16
F32 = jnp.float32
MESH = pl.DeviceIdType.MESH

courant = 0.1
VMEM_LIMIT = 48 * 2**20
ORDER = (4, 5, 3, 6, 2, 7, 1, 12, 13, 11, 14, 10, 15, 9, 8)
RIGHT_LEFT = float(sum((-1) ** order * (2 * order + 1) / 2.0 for order in range(4)))


def legendre(order, points):
    values = np.asarray(points) * 1.0
    if order == 0:
        poly = values * 0.0 + 1.0
    elif order == 1:
        poly = values
    elif order == 2:
        poly = (3.0 * values * values - 1.0) / 2.0
    else:
        poly = (5.0 * values * values * values - 3.0 * values) / 2.0
    return np.sqrt((2 * order + 1) / 2.0) * poly


def line_tables():
    nodes = np.array(
        [-0.8611363115940526, -0.3399810435848563, 0.3399810435848563, 0.8611363115940526]
    )
    weights = np.array(
        [0.3478548451374538, 0.6521451548625461, 0.6521451548625461, 0.3478548451374538]
    )
    stiff = np.zeros((4, 4))
    coarse = np.zeros((4, 8))
    for row in range(4):
        for column in range(4):
            if column < row and (row + column) % 2 == 1:
                stiff[row, column] = np.sqrt((2.0 * row + 1.0) * (2.0 * column + 1.0))
            coarse[row, column] = np.sum(
                weights * legendre(row, (nodes - 1.0) / 2.0) * legendre(column, nodes)
            ) / np.sqrt(2.0)
            coarse[row, column + 4] = np.sum(
                weights * legendre(row, (nodes + 1.0) / 2.0) * legendre(column, nodes)
            ) / np.sqrt(2.0)
    right = np.array([float(legendre(order, 1.0)) for order in range(4)])
    left = np.array([float(legendre(order, -1.0)) for order in range(4)])
    rows = [coarse[index] for index in range(4)]
    for index in range(4, 8):
        vector = np.eye(8)[index]
        for other in rows:
            vector = vector - np.dot(other, vector) * other
        rows.append(vector / np.sqrt(np.sum(vector * vector)))
    return (stiff - np.outer(right, right), right, left, np.array(rows))


def along(matrix, axis):
    return np.kron(np.eye(4**axis), np.kron(matrix, np.eye(4 ** (2 - axis))))


def twice(matrix):
    return np.kron(np.eye(2), matrix)


def first_basis():
    interior, _, left, _ = line_tables()
    turned, _ = np.linalg.qr(np.stack([left, interior @ left], axis=1), mode="complete")
    return np.concatenate([turned[:, 2:], turned[:, :2]], axis=1).T


def split_table(table):
    hi = table.astype(ml_dtypes.bfloat16)
    lo = (table - hi.astype(np.float64)).astype(ml_dtypes.bfloat16)
    return np.stack([hi, lo], axis=-3)


def line_hierarchy(filters, rise):
    cells = 2**rise
    whole = np.eye(cells * 4).reshape(cells, 4, cells * 4)
    for level_step in range(rise):
        for first in range(0, cells, 2 ** (level_step + 1)):
            second = first + 2**level_step
            pair = np.concatenate([whole[first], whole[second]], axis=0)
            mixed = filters @ pair
            whole[first], whole[second] = mixed[:4], mixed[4:]
    ordered = np.zeros_like(whole)
    for low in range(cells):
        digit = 0
        if low > 0:
            zeros = (low & -low).bit_length() - 1
            height = rise - zeros
            digit = 2 ** (height - 1) + (low >> (zeros + 1))
        ordered[digit] = whole[low]
    return ordered.reshape(cells, 4, cells, 4)


def compositions():
    return [(a, b, RISE - a - b) for a in range(RISE + 1) for b in range(RISE + 1 - a)]


@functools.lru_cache(None)
def tables():
    interior, right, left, filters = line_tables()
    stiff = np.stack([twice(along(interior, axis).T) for axis in range(3)]).astype(np.float32)
    lift = np.zeros((128, 128), np.float32)
    trace = np.zeros((128, 128))
    for axis in range(3):
        lift[32 * axis : 32 * (axis + 1)] = twice(along(left[:, None], axis).T)
        trace[:, 32 * axis : 32 * (axis + 1)] = twice(along(right[None, :], axis).T)
    lines = [line_hierarchy(filters, rise) for rise in range(RISE + 1)]
    hier = []
    for one, two, three in compositions():
        whole = np.einsum("aqlp,brms,cuno->qruabclmnpso", lines[one], lines[two], lines[three])
        hier.append(whole.reshape(GRID, GRID))
    hi, lo = split_table(trace)
    trace = np.block([[hi, lo], [hi, np.zeros_like(lo)]])
    return stiff, lift, trace, split_table(np.stack(hier))


def split(values):
    hi = values.astype(BF16)
    return hi, (values - hi.astype(F32)).astype(BF16)


def dot(one, two):
    return jnp.dot(one, two, preferred_element_type=F32)


def dot_nt(one, two):
    return lax.dot_general(one, two, (((1,), (1,)), ((), ())), preferred_element_type=F32)


def fold(values):
    return values[:, :128] + values[:, 128:]


def square(matrix):
    hi, lo = split(matrix)
    zero = jnp.zeros_like(lo)
    return jnp.concatenate(
        [jnp.concatenate([hi, lo], axis=1), jnp.concatenate([hi, zero], axis=1)], axis=0
    )


def kernel(
    comps,
    shards,
    levels_hbm,
    coefs_hbm,
    velocity_hbm,
    x_hbm,
    stiff_hbm,
    lift_hbm,
    trace_hbm,
    hier_hbm,
    out_ref,
    levels,
    coefs,
    velocity,
    x_v,
    stiff_v,
    lift_v,
    trace_v,
    hier_v,
    onehot,
    match,
    wide,
    lifts,
    field,
    other,
    traces,
    shifted,
    plane,
    edge_out,
    edge_in,
    rows,
    sent,
    got,
    back,
    home,
    local_sem,
    edge_send,
    edge_recv,
    there_send,
    there_recv,
    back_send,
    back_recv,
):
    me = lax.axis_index("comp")
    spot = lax.axis_index("shard")
    ahead = lax.rem(spot + 1, shards)
    behind = lax.rem(spot + shards - 1, shards)

    def fetch(source, target, index):
        copy = pltpu.make_async_copy(source, target, local_sem.at[index])
        copy.start()
        return copy

    levels_copy = fetch(levels_hbm, levels, 0)
    x_copy = fetch(x_hbm.at[0, 0], x_v, 1)
    velocity_copy = fetch(velocity_hbm, velocity, 2)
    trace_copy = fetch(trace_hbm, trace_v, 3)
    stiff_copy = fetch(stiff_hbm, stiff_v, 4)
    lift_copy = fetch(lift_hbm, lift_v, 5)
    coefs_copy = fetch(coefs_hbm, coefs, 6)
    hier_copy = fetch(hier_hbm, hier_v, 7)

    barrier = pltpu.get_barrier_semaphore()
    for step in range(1, comps):
        pl.semaphore_signal(
            barrier, inc=1, device_id={"comp": lax.rem(me + step, comps)}, device_id_type=MESH
        )
    pl.semaphore_signal(barrier, inc=1, device_id={"shard": behind}, device_id_type=MESH)

    levels_copy.wait()

    def rise_of(comp, axis):
        return jnp.clip(levels[axis, comp] - BASE, 0, RISE)

    rise1 = rise_of(me, 0)
    rise2 = rise_of(me, 1)
    rise3 = rise_of(me, 2)
    kind = jnp.clip(lax.shift_right_logical(rise1 * (9 - rise1), 1) + rise2, 0, KINDS - 1)
    one = jnp.int32(1)

    def low_digits(low):
        low3 = low & (lax.shift_left(one, rise3) - 1)
        low2 = lax.shift_right_logical(low, rise3) & (lax.shift_left(one, rise2) - 1)
        low1 = lax.shift_right_logical(low, rise2 + rise3)
        return low1, low2, low3

    def cell_of(digit1, digit2, digit3):
        return (
            lax.shift_left(digit1, rise2 + rise3 + 2 * BASE)
            + lax.shift_left(digit2, rise3 + BASE)
            + digit3
        )

    offsets = [cell_of(*low_digits(jnp.int32(low))) for low in range(LOW)]

    def place_cell(place):
        return cell_of(
            lax.shift_left(lax.shift_right_logical(place, 4) & 3, jnp.full(place.shape, rise1)),
            lax.shift_left(lax.shift_right_logical(place, 2) & 3, jnp.full(place.shape, rise2)),
            lax.shift_left(place & 3, jnp.full(place.shape, rise3)),
        )

    place_row = lax.broadcasted_iota(jnp.int32, (PLACES, 128), 0)
    lanes = lax.broadcasted_iota(jnp.int32, (PLACES, 128), 1)
    left_half = lanes < 64
    place_rows = place_cell(place_row)
    for low in range(LOW):
        for part in range(GRID // 128):
            hit = (place_rows + offsets[low]) == (lanes + 128 * part)
            onehot[low * PLACES : (low + 1) * PLACES, 128 * part : 128 * (part + 1)] = jnp.where(
                hit, 1.0, 0.0
            ).astype(BF16)

    def halves(one, two):
        return jnp.where(left_half, one, two)

    def swap(values):
        return pltpu.roll(values, 64, 1)

    def block_of(low):
        return slice(low * PLACES, (low + 1) * PLACES)

    def blocks(values):
        return [values[block_of(low), :] for low in range(LOW)]

    x_copy.wait()
    hi, lo = split(x_v[...])
    now = dot(onehot[...], hi) + dot(onehot[...], lo)
    field[...] = now
    other[:, :128] = swap(now[:, :128])
    other[:, 128:] = swap(now[:, 128:])

    basis = first_basis()
    interior, right, left, _ = line_tables()

    def pair_of(rows_of):
        return [
            jnp.where(left_half[:1], float(rows_of[0][first]), float(rows_of[1][second]))
            for first, second in ((0, 1), (1, 0), (2, 3), (3, 2))
        ]

    def mix(factors):
        return (
            factors[0] * field[:, :128]
            + factors[1] * other[:, :128]
            + factors[2] * field[:, 128:]
            + factors[3] * other[:, 128:]
        )

    def edge_copy(stage):
        return pltpu.make_async_remote_copy(
            src_ref=edge_out.at[stage],
            dst_ref=edge_in.at[stage],
            send_sem=edge_send.at[stage],
            recv_sem=edge_recv.at[stage],
            device_id={"shard": ahead},
            device_id_type=MESH,
        )

    def pack(stage, values):
        parts = blocks(values)
        for low in range(LOW // 2):
            edge_out[stage, low] = halves(parts[low], parts[low + LOW // 2])

    pack(0, mix(pair_of([right, right])))
    pl.semaphore_wait(barrier, comps)
    first_edge, second_edge = edge_copy(0), edge_copy(1)
    first_edge.start()

    velocity_copy.wait()
    reach = None
    for comp in range(comps):
        total = velocity[0] * (1.0 * shards)
        for axis in range(3):
            size = lax.shift_left(one, levels[axis, comp]).astype(F32)
            total = total + velocity[axis + 1] * size
        reach = total if reach is None else jnp.maximum(reach, total)
    step_size = jnp.full((1, 128), courant, F32) / jnp.full((1, 128), reach, F32)
    sizes = [jnp.float32(shards)] + [
        lax.shift_left(one, levels[axis, me]).astype(F32) for axis in range(3)
    ]
    first_scale, *scales = [
        step_size * (2.0 * velocity[axis] * sizes[axis]) for axis in range(4)
    ]
    stiff_copy.wait()
    wide[...] = square(
        scales[0] * stiff_v[0] + scales[1] * stiff_v[1] + scales[2] * stiff_v[2]
    )
    lift_copy.wait()
    scale_rows = [jnp.broadcast_to(scale, (32, 128)) for scale in scales]
    lifts[...] = square(
        jnp.concatenate([*scale_rows, jnp.zeros((32, 128), F32)], axis=0) * lift_v[...]
    )

    def behind_of(low, axis):
        digits = list(low_digits(jnp.int32(low)))
        rise = (rise1, rise2, rise3)[axis]
        first = digits[axis] == 0
        digits[axis] = (digits[axis] + lax.shift_left(one, rise) - 1) & (
            lax.shift_left(one, rise) - 1
        )
        spot = (
            lax.shift_left(digits[0], rise2 + rise3) + lax.shift_left(digits[1], rise3) + digits[2]
        )
        return (spot & (LOW - 1)) + jnp.where(first, LOW, 0)

    sources = [[behind_of(low, axis) for axis in range(3)] for low in range(LOW)]

    def by_axis(one, two, three):
        return jnp.where(lanes < 32, one, jnp.where(lanes < 64, two, three))

    def others_step(values):
        pair = jnp.concatenate(split(values), axis=1)
        for low, now in enumerate(blocks(fold(dot(pair, trace_v[...])))):
            traces[low] = now
            traces[LOW + low] = by_axis(
                pltpu.roll(now, 16, 0),
                jnp.where(
                    (place_row & 15) < 4, pltpu.roll(now, PLACES - 12, 0), pltpu.roll(now, 4, 0)
                ),
                jnp.where(
                    (place_row & 3) < 1, pltpu.roll(now, PLACES - 3, 0), pltpu.roll(now, 1, 0)
                ),
            )
        inner = dot(pair, wide[...])
        for low in range(LOW):
            shifted[block_of(low), :] = by_axis(*[traces[source] for source in sources[low]])
        return fold(inner + dot(jnp.concatenate(split(shifted[...]), axis=1), lifts[...]))

    def combinations(half):
        plain, once, square_of = [
            pair_of(matrix[2 * half : 2 * half + 2])
            for matrix in (basis, basis @ interior, basis @ interior @ interior)
        ]
        step = first_scale
        return (
            mix(plain),
            mix([2.0 * (p + step * o) for p, o in zip(plain, once)]),
            mix([p + step * (o + 0.5 * step * q) for p, o, q in zip(plain, once, square_of)]),
        )

    def edge_at(stage, low):
        edge = edge_in[stage, low % (LOW // 2)]
        turned = swap(edge)
        return halves(edge, turned) if low < LOW // 2 else halves(turned, edge)

    pack(1, mix([first_scale * part for part in pair_of([right @ interior] * 2)]))

    def exchange(source, target, half, send_sem, recv_sem):
        copies = []
        for step in ORDER:
            other = lax.rem(me + step, comps)
            copy = pltpu.make_async_remote_copy(
                src_ref=source.at[half, other],
                dst_ref=target.at[half, me],
                send_sem=send_sem.at[half, step],
                recv_sem=recv_sem.at[half, step],
                device_id={"comp": other},
                device_id_type=MESH,
            )
            copy.start()
            copies.append(copy)
        target[half, me] = source[half, me]
        return copies

    def to_owners(half, advanced):
        parts = blocks(advanced)
        for pair in range(LOW // 2):
            even, odd = parts[2 * pair], parts[2 * pair + 1]
            into = slice(128 * pair, 128 * (pair + 1))
            hi, lo = split(jnp.concatenate([halves(even, swap(odd)), halves(swap(even), odd)]))
            rows[half, :128, into] = hi
            rows[half, 128:, into] = lo
        both = dot_nt(h_hi, rows[half])
        whole = fold(both) + dot_nt(h_lo, rows[half, :128])
        sent[half] = whole.reshape(sent.shape[1:])
        return exchange(sent, got, half, there_send, there_recv)

    def pass_edge():
        first_edge.wait()
        for low in range(LOW // 2):
            edge_out[1, low] += (first_scale * RIGHT_LEFT) * edge_in[0, low]
        second_edge.start()

    trace_copy.wait()
    y, m, u = combinations(0)
    advanced = u + 0.5 * others_step(m + others_step(y))
    hier_copy.wait()
    h_hi, h_lo = hier_v[kind, 0], hier_v[kind, 1]
    there = [to_owners(0, advanced)]

    pass_edge()
    y, m, u = combinations(1)
    bent = basis @ interior @ left
    straight = float(basis[2] @ left)
    to_m = jnp.where(left_half[:1], 2.0 * straight * first_scale, 0.0)
    to_u = first_scale * jnp.where(
        left_half[:1],
        straight + 0.5 * float(bent[2]) * first_scale,
        0.5 * float(bent[3]) * first_scale,
    )
    to_u2 = jnp.where(left_half[:1], 0.5 * straight * first_scale, 0.0)
    edges = jnp.concatenate([edge_at(0, low) for low in range(LOW)], axis=0)
    plane[...] = u + to_u * edges + 0.5 * others_step(m + to_m * edges + others_step(y))
    second_edge.wait()
    edges = jnp.concatenate([edge_at(1, low) for low in range(LOW)], axis=0)
    there.append(to_owners(1, plane[...] + to_u2 * edges))

    coefs_copy.wait()

    def code_of(digits, comp):
        up2 = rise_of(comp, 1)
        up3 = rise_of(comp, 2)
        digit3 = digits & (lax.shift_left(one, up3) - 1)
        digit2 = lax.shift_right_logical(digits, jnp.full(digits.shape, up3)) & (
            lax.shift_left(one, up2) - 1
        )
        digit1 = lax.shift_right_logical(digits, jnp.full(digits.shape, up2 + up3))
        return digit1 * 64 + digit2 * 8 + digit3

    piece_row = lax.broadcasted_iota(jnp.int32, (8, 128), 0)
    piece_lane = lax.broadcasted_iota(jnp.int32, (8, 128), 1)
    lane_code = jnp.zeros((8, 128), jnp.int32)
    lane_coef = jnp.zeros((8, 128), F32)
    for comp in range(comps):
        own = lax.shift_right_logical(piece_lane, 3) == comp
        lane_code = jnp.where(own, code_of(piece_lane & 7, comp), lane_code)
        lane_coef = jnp.where(own, jnp.full((8, 128), coefs[comp].astype(F32)), lane_coef)
    for comp in range(0, comps, 2):
        block = [
            jnp.where(code_of(piece_row, here) == lane_code, lane_coef, 0.0)
            for here in (comp, comp + 1)
        ]
        match[8 * comp : 8 * comp + 16, :] = jnp.concatenate(block, axis=0).astype(BF16)

    cell_rows = lax.broadcasted_iota(jnp.int32, (GRID, 128), 0)
    lane_place = place_cell(piece_lane & (PLACES - 1))
    for part in range(GRID // 128):
        lane_cell = lane_place + jnp.where(
            piece_lane < 64, offsets[2 * part], offsets[2 * part + 1]
        )
        onehot[:, 128 * part : 128 * (part + 1)] = jnp.where(
            cell_rows == lane_cell[0:1, :], 1.0, 0.0
        ).astype(BF16)

    homeward = []
    for half in range(2):
        for copy in there[half]:
            copy.wait()
        for quarter in range(4):
            part = slice(8 * quarter, 8 * (quarter + 1))
            hi, lo = split(got[half, :, part, :].reshape(8 * comps, 128))
            both = dot(match[...], jnp.concatenate([hi, lo], axis=1))
            back[half, :, part, :] = fold(both).reshape(comps, 8, 128)
        homeward.append(exchange(back, home, half, back_send, back_recv))

    for half in range(2):
        for copy in homeward[half]:
            copy.wait()
        hi, lo = split(home[half].reshape(GRID, 128).T)
        both = dot(jnp.concatenate([hi, lo]), h_hi)
        plain = both[:128] + both[128:] + dot(hi, h_lo)
        for pair in range(LOW // 2):
            into = slice(128 * pair, 128 * (pair + 1))
            upper, lower = plain[:64, into], plain[64:, into]
            plane[block_of(2 * pair), :] = halves(upper, swap(lower))
            plane[block_of(2 * pair + 1), :] = halves(swap(upper), lower)
        pair = jnp.concatenate(split(plane[...]), axis=1)
        for part in range(4):
            cells = slice(128 * part, 128 * (part + 1))
            turned = fold(dot(onehot[cells, :], pair))
            swapped = swap(turned)
            for group in range(2):
                near = [float(basis[2 * half + k, 2 * group + k]) for k in range(2)]
                far = [float(basis[2 * half + 1 - k, 2 * group + k]) for k in range(2)]
                value = (
                    jnp.where(left_half[:1], near[0], near[1]) * turned
                    + jnp.where(left_half[:1], far[0], far[1]) * swapped
                )
                columns = slice(128 * group, 128 * (group + 1))
                if half == 0:
                    out_ref[0, 0, cells, columns] = value
                else:
                    out_ref[0, 0, cells, columns] += value


def on_device(modal_coefs, comp_levels, comp_coefs, velocity):
    comps = lax.axis_size("comp")
    shards = lax.axis_size("shard")
    stiff, lift, trace, hier = tables()
    anywhere = pl.BlockSpec(memory_space=pl.ANY)
    dma = pltpu.SemaphoreType.DMA
    exchanged = pltpu.VMEM((2, comps, GRID // comps, 128), F32)
    return pl.pallas_call(
        functools.partial(kernel, comps, shards),
        out_shape=pltpu.VMEM(modal_coefs.shape, F32),
        in_specs=[anywhere] * 8,
        out_specs=pl.BlockSpec(memory_space=pltpu.VMEM),
        scratch_shapes=[
            pltpu.SMEM((3, comps), jnp.int32),
            pltpu.SMEM((comps,), jnp.int32),
            pltpu.SMEM((4,), F32),
            pltpu.VMEM((GRID, COEF), F32),
            pltpu.VMEM(stiff.shape, F32),
            pltpu.VMEM(lift.shape, F32),
            pltpu.VMEM(trace.shape, BF16),
            pltpu.VMEM(hier.shape, BF16),
            pltpu.VMEM((GRID, GRID), BF16),
            pltpu.VMEM((8 * comps, 8 * comps), BF16),
            pltpu.VMEM((COEF, COEF), BF16),
            pltpu.VMEM((COEF, COEF), BF16),
            pltpu.VMEM((GRID, COEF), F32),
            pltpu.VMEM((GRID, COEF), F32),
            pltpu.VMEM((2 * LOW, PLACES, 128), F32),
            pltpu.VMEM((GRID, 128), F32),
            pltpu.VMEM((GRID, 128), F32),
            pltpu.VMEM((2, LOW // 2, PLACES, 128), F32),
            pltpu.VMEM((2, LOW // 2, PLACES, 128), F32),
            pltpu.VMEM((2, 2 * 128, GRID), BF16),
            exchanged,
            exchanged,
            exchanged,
            exchanged,
            dma((8,)),
            dma((2,)),
            dma((2,)),
            dma((2, comps)),
            dma((2, comps)),
            dma((2, comps)),
            dma((2, comps)),
        ],
        compiler_params=pltpu.CompilerParams(
            collective_id=0, has_side_effects=True, vmem_limit_bytes=VMEM_LIMIT
        ),
        name="combine",
    )(
        *[
            pltpu.with_memory_space_constraint(array, pltpu.HBM)
            for array in (
                comp_levels.T,
                comp_coefs,
                velocity,
                modal_coefs,
                jnp.asarray(stiff),
                jnp.asarray(lift),
                jnp.asarray(trace),
                jnp.asarray(hier),
            )
        ]
    )


def solution(mesh):
    placed = (P("comp", "shard", None, None), P(), P(), P())
    return jax.shard_map(
        on_device,
        mesh=mesh,
        in_specs=placed,
        out_specs=P("comp", "shard", None, None),
        check_vma=False,
    )
```

```python
import functools

import jax
import jax.numpy as jnp
import ml_dtypes
import numpy as np
from jax import lax
from jax.experimental import pallas as pl
from jax.experimental.pallas import tpu as pltpu
from jax.sharding import PartitionSpec as P

COEF = 256
BASE = 2
RISE = 3
GRID = 512
LOW = 2**RISE
PLACES = (2**BASE) ** 3
KINDS = (RISE + 1) * (RISE + 2) // 2
BF16 = jnp.bfloat16
F32 = jnp.float32
MESH = pl.DeviceIdType.MESH

courant = 0.1
VMEM_LIMIT = 48 * 2**20
ORDER = (4, 5, 3, 6, 2, 7, 1, 12, 13, 11, 14, 10, 15, 9, 8)
RIGHT_LEFT = float(sum((-1) ** order * (2 * order + 1) / 2.0 for order in range(4)))


def legendre(order, points):
    values = np.asarray(points) * 1.0
    if order == 0:
        poly = values * 0.0 + 1.0
    elif order == 1:
        poly = values
    elif order == 2:
        poly = (3.0 * values * values - 1.0) / 2.0
    else:
        poly = (5.0 * values * values * values - 3.0 * values) / 2.0
    return np.sqrt((2 * order + 1) / 2.0) * poly


def line_tables():
    nodes = np.array(
        [-0.8611363115940526, -0.3399810435848563, 0.3399810435848563, 0.8611363115940526]
    )
    weights = np.array(
        [0.3478548451374538, 0.6521451548625461, 0.6521451548625461, 0.3478548451374538]
    )
    stiff = np.zeros((4, 4))
    coarse = np.zeros((4, 8))
    for row in range(4):
        for column in range(4):
            if column < row and (row + column) % 2 == 1:
                stiff[row, column] = np.sqrt((2.0 * row + 1.0) * (2.0 * column + 1.0))
            coarse[row, column] = np.sum(
                weights * legendre(row, (nodes - 1.0) / 2.0) * legendre(column, nodes)
            ) / np.sqrt(2.0)
            coarse[row, column + 4] = np.sum(
                weights * legendre(row, (nodes + 1.0) / 2.0) * legendre(column, nodes)
            ) / np.sqrt(2.0)
    right = np.array([float(legendre(order, 1.0)) for order in range(4)])
    left = np.array([float(legendre(order, -1.0)) for order in range(4)])
    rows = [coarse[index] for index in range(4)]
    for index in range(4, 8):
        vector = np.eye(8)[index]
        for other in rows:
            vector = vector - np.dot(other, vector) * other
        rows.append(vector / np.sqrt(np.sum(vector * vector)))
    return (stiff - np.outer(right, right), right, left, np.array(rows))


def along(matrix, axis):
    return np.kron(np.eye(4**axis), np.kron(matrix, np.eye(4 ** (2 - axis))))


def twice(matrix):
    return np.kron(np.eye(2), matrix)


def first_basis():
    interior, _, left, _ = line_tables()
    turned, _ = np.linalg.qr(np.stack([left, interior @ left], axis=1), mode="complete")
    return np.concatenate([turned[:, 2:], turned[:, :2]], axis=1).T


def split_table(table):
    hi = table.astype(ml_dtypes.bfloat16)
    lo = (table - hi.astype(np.float64)).astype(ml_dtypes.bfloat16)
    return np.stack([hi, lo], axis=-3)


def line_hierarchy(filters, rise):
    cells = 2**rise
    whole = np.eye(cells * 4).reshape(cells, 4, cells * 4)
    for level_step in range(rise):
        for first in range(0, cells, 2 ** (level_step + 1)):
            second = first + 2**level_step
            pair = np.concatenate([whole[first], whole[second]], axis=0)
            mixed = filters @ pair
            whole[first], whole[second] = mixed[:4], mixed[4:]
    ordered = np.zeros_like(whole)
    for low in range(cells):
        digit = 0
        if low > 0:
            zeros = (low & -low).bit_length() - 1
            height = rise - zeros
            digit = 2 ** (height - 1) + (low >> (zeros + 1))
        ordered[digit] = whole[low]
    return ordered.reshape(cells, 4, cells, 4)


def compositions():
    return [(a, b, RISE - a - b) for a in range(RISE + 1) for b in range(RISE + 1 - a)]


@functools.lru_cache(None)
def tables():
    interior, right, left, filters = line_tables()
    stiff = np.stack([twice(along(interior, axis).T) for axis in range(3)]).astype(np.float32)
    lift = np.zeros((128, 128), np.float32)
    trace = np.zeros((128, 128))
    for axis in range(3):
        lift[32 * axis : 32 * (axis + 1)] = twice(along(left[:, None], axis).T)
        trace[:, 32 * axis : 32 * (axis + 1)] = twice(along(right[None, :], axis).T)
    lines = [line_hierarchy(filters, rise) for rise in range(RISE + 1)]
    hier = []
    for one, two, three in compositions():
        whole = np.einsum("aqlp,brms,cuno->qruabclmnpso", lines[one], lines[two], lines[three])
        hier.append(whole.reshape(GRID, GRID))
    hi, lo = split_table(trace)
    trace = np.block([[hi, lo], [hi, np.zeros_like(lo)]])
    return stiff, lift, trace, split_table(np.stack(hier))


def split(values):
    hi = values.astype(BF16)
    return hi, (values - hi.astype(F32)).astype(BF16)


def dot(one, two):
    return jnp.dot(one, two, preferred_element_type=F32)


def dot_nt(one, two):
    return lax.dot_general(one, two, (((1,), (1,)), ((), ())), preferred_element_type=F32)


def fold(values):
    return values[:, :128] + values[:, 128:]


def square(matrix):
    hi, lo = split(matrix)
    zero = jnp.zeros_like(lo)
    return jnp.concatenate(
        [jnp.concatenate([hi, lo], axis=1), jnp.concatenate([hi, zero], axis=1)], axis=0
    )


def kernel(
    comps,
    shards,
    levels_hbm,
    coefs_hbm,
    velocity_hbm,
    x_hbm,
    stiff_hbm,
    lift_hbm,
    trace_hbm,
    hier_hbm,
    out_ref,
    levels,
    coefs,
    velocity,
    x_v,
    stiff_v,
    lift_v,
    trace_v,
    hier_v,
    onehot,
    match,
    wide,
    lifts,
    field,
    other,
    traces,
    shifted,
    plane,
    edge_out,
    edge_in,
    rows,
    sent,
    got,
    back,
    home,
    local_sem,
    edge_send,
    edge_recv,
    there_send,
    there_recv,
    back_send,
    back_recv,
):
    me = lax.axis_index("comp")
    spot = lax.axis_index("shard")
    ahead = lax.rem(spot + 1, shards)
    behind = lax.rem(spot + shards - 1, shards)

    def fetch(source, target, index):
        copy = pltpu.make_async_copy(source, target, local_sem.at[index])
        copy.start()
        return copy

    levels_copy = fetch(levels_hbm, levels, 0)
    x_copy = fetch(x_hbm.at[0, 0], x_v, 1)
    velocity_copy = fetch(velocity_hbm, velocity, 2)
    trace_copy = fetch(trace_hbm, trace_v, 3)
    stiff_copy = fetch(stiff_hbm, stiff_v, 4)
    lift_copy = fetch(lift_hbm, lift_v, 5)
    coefs_copy = fetch(coefs_hbm, coefs, 6)
    hier_copy = fetch(hier_hbm, hier_v, 7)

    barrier = pltpu.get_barrier_semaphore()
    for step in range(1, comps):
        pl.semaphore_signal(
            barrier, inc=1, device_id={"comp": lax.rem(me + step, comps)}, device_id_type=MESH
        )
    pl.semaphore_signal(barrier, inc=1, device_id={"shard": behind}, device_id_type=MESH)

    levels_copy.wait()

    def rise_of(comp, axis):
        return jnp.clip(levels[axis, comp] - BASE, 0, RISE)

    rise1 = rise_of(me, 0)
    rise2 = rise_of(me, 1)
    rise3 = rise_of(me, 2)
    kind = jnp.clip(lax.shift_right_logical(rise1 * (9 - rise1), 1) + rise2, 0, KINDS - 1)
    one = jnp.int32(1)

    def low_digits(low):
        low3 = low & (lax.shift_left(one, rise3) - 1)
        low2 = lax.shift_right_logical(low, rise3) & (lax.shift_left(one, rise2) - 1)
        low1 = lax.shift_right_logical(low, rise2 + rise3)
        return low1, low2, low3

    def cell_of(digit1, digit2, digit3):
        return (
            lax.shift_left(digit1, rise2 + rise3 + 2 * BASE)
            + lax.shift_left(digit2, rise3 + BASE)
            + digit3
        )

    offsets = [cell_of(*low_digits(jnp.int32(low))) for low in range(LOW)]

    def place_cell(place):
        return cell_of(
            lax.shift_left(lax.shift_right_logical(place, 4) & 3, jnp.full(place.shape, rise1)),
            lax.shift_left(lax.shift_right_logical(place, 2) & 3, jnp.full(place.shape, rise2)),
            lax.shift_left(place & 3, jnp.full(place.shape, rise3)),
        )

    place_row = lax.broadcasted_iota(jnp.int32, (PLACES, 128), 0)
    lanes = lax.broadcasted_iota(jnp.int32, (PLACES, 128), 1)
    left_half = lanes < 64
    place_rows = place_cell(place_row)
    for low in range(LOW):
        for part in range(GRID // 128):
            hit = (place_rows + offsets[low]) == (lanes + 128 * part)
            onehot[low * PLACES : (low + 1) * PLACES, 128 * part : 128 * (part + 1)] = jnp.where(
                hit, 1.0, 0.0
            ).astype(BF16)

    def halves(one, two):
        return jnp.where(left_half, one, two)

    def swap(values):
        return pltpu.roll(values, 64, 1)

    def block_of(low):
        return slice(low * PLACES, (low + 1) * PLACES)

    def blocks(values):
        return [values[block_of(low), :] for low in range(LOW)]

    x_copy.wait()
    hi, lo = split(x_v[...])
    now = dot(onehot[...], hi) + dot(onehot[...], lo)
    field[...] = now
    other[:, :128] = swap(now[:, :128])
    other[:, 128:] = swap(now[:, 128:])

    basis = first_basis()
    interior, right, left, _ = line_tables()

    def pair_of(rows_of):
        return [
            jnp.where(left_half[:1], float(rows_of[0][first]), float(rows_of[1][second]))
            for first, second in ((0, 1), (1, 0), (2, 3), (3, 2))
        ]

    def mix(factors):
        return (
            factors[0] * field[:, :128]
            + factors[1] * other[:, :128]
            + factors[2] * field[:, 128:]
            + factors[3] * other[:, 128:]
        )

    def edge_copy(stage):
        return pltpu.make_async_remote_copy(
            src_ref=edge_out.at[stage],
            dst_ref=edge_in.at[stage],
            send_sem=edge_send.at[stage],
            recv_sem=edge_recv.at[stage],
            device_id={"shard": ahead},
            device_id_type=MESH,
        )

    def pack(stage, values):
        parts = blocks(values)
        for low in range(LOW // 2):
            edge_out[stage, low] = halves(parts[low], parts[low + LOW // 2])

    pack(0, mix(pair_of([right, right])))
    pl.semaphore_wait(barrier, comps)
    first_edge, second_edge = edge_copy(0), edge_copy(1)
    first_edge.start()

    velocity_copy.wait()
    reach = None
    for comp in range(comps):
        total = velocity[0] * (1.0 * shards)
        for axis in range(3):
            size = lax.shift_left(one, levels[axis, comp]).astype(F32)
            total = total + velocity[axis + 1] * size
        reach = total if reach is None else jnp.maximum(reach, total)
    step_size = jnp.full((1, 128), courant, F32) / jnp.full((1, 128), reach, F32)
    sizes = [jnp.float32(shards)] + [
        lax.shift_left(one, levels[axis, me]).astype(F32) for axis in range(3)
    ]
    first_scale, *scales = [
        step_size * (2.0 * velocity[axis] * sizes[axis]) for axis in range(4)
    ]
    stiff_copy.wait()
    wide[...] = square(
        scales[0] * stiff_v[0] + scales[1] * stiff_v[1] + scales[2] * stiff_v[2]
    )
    lift_copy.wait()
    scale_rows = [jnp.broadcast_to(scale, (32, 128)) for scale in scales]
    lifts[...] = square(
        jnp.concatenate([*scale_rows, jnp.zeros((32, 128), F32)], axis=0) * lift_v[...]
    )

    def behind_of(low, axis):
        digits = list(low_digits(jnp.int32(low)))
        rise = (rise1, rise2, rise3)[axis]
        first = digits[axis] == 0
        digits[axis] = (digits[axis] + lax.shift_left(one, rise) - 1) & (
            lax.shift_left(one, rise) - 1
        )
        spot = (
            lax.shift_left(digits[0], rise2 + rise3) + lax.shift_left(digits[1], rise3) + digits[2]
        )
        return (spot & (LOW - 1)) + jnp.where(first, LOW, 0)

    sources = [[behind_of(low, axis) for axis in range(3)] for low in range(LOW)]

    def by_axis(one, two, three):
        return jnp.where(lanes < 32, one, jnp.where(lanes < 64, two, three))

    def others_step(values):
        pair = jnp.concatenate(split(values), axis=1)
        for low, now in enumerate(blocks(fold(dot(pair, trace_v[...])))):
            traces[low] = now
            traces[LOW + low] = by_axis(
                pltpu.roll(now, 16, 0),
                jnp.where(
                    (place_row & 15) < 4, pltpu.roll(now, PLACES - 12, 0), pltpu.roll(now, 4, 0)
                ),
                jnp.where(
                    (place_row & 3) < 1, pltpu.roll(now, PLACES - 3, 0), pltpu.roll(now, 1, 0)
                ),
            )
        inner = dot(pair, wide[...])
        for low in range(LOW):
            shifted[block_of(low), :] = by_axis(*[traces[source] for source in sources[low]])
        return fold(inner + dot(jnp.concatenate(split(shifted[...]), axis=1), lifts[...]))

    def combinations(half):
        plain, once, square_of = [
            pair_of(matrix[2 * half : 2 * half + 2])
            for matrix in (basis, basis @ interior, basis @ interior @ interior)
        ]
        step = first_scale
        return (
            mix(plain),
            mix([2.0 * (p + step * o) for p, o in zip(plain, once)]),
            mix([p + step * (o + 0.5 * step * q) for p, o, q in zip(plain, once, square_of)]),
        )

    def edge_at(stage, low):
        edge = edge_in[stage, low % (LOW // 2)]
        turned = swap(edge)
        return halves(edge, turned) if low < LOW // 2 else halves(turned, edge)

    pack(1, mix([first_scale * part for part in pair_of([right @ interior] * 2)]))

    def exchange(source, target, half, send_sem, recv_sem, turns=()):
        copies = []
        for step in ORDER:
            other = lax.rem(me + step, comps)
            copy = pltpu.make_async_remote_copy(
                src_ref=source.at[half, other],
                dst_ref=target.at[half, me],
                send_sem=send_sem.at[half, step],
                recv_sem=recv_sem.at[half, step],
                device_id={"comp": other},
                device_id_type=MESH,
            )
            copies.append((copy, lax.rem(other, 8)))
        for first, last in turns or [(0, 8)]:
            for copy, height in copies:
                if turns:
                    pl.when((height >= first) & (height < last))(copy.start)
                else:
                    copy.start()
        target[half, me] = source[half, me]
        return [copy for copy, _ in copies]

    def to_owners(half, advanced):
        parts = blocks(advanced)
        for pair in range(LOW // 2):
            even, odd = parts[2 * pair], parts[2 * pair + 1]
            into = slice(128 * pair, 128 * (pair + 1))
            hi, lo = split(jnp.concatenate([halves(even, swap(odd)), halves(swap(even), odd)]))
            rows[half, :128, into] = hi
            rows[half, 128:, into] = lo
        both = dot_nt(h_hi, rows[half])
        whole = fold(both) + dot_nt(h_lo, rows[half, :128])
        sent[half] = whole.reshape(sent.shape[1:])
        return exchange(sent, got, half, there_send, there_recv)

    def pass_edge():
        first_edge.wait()
        for low in range(LOW // 2):
            edge_out[1, low] += (first_scale * RIGHT_LEFT) * edge_in[0, low]
        second_edge.start()

    trace_copy.wait()
    y, m, u = combinations(0)
    advanced = u + 0.5 * others_step(m + others_step(y))
    hier_copy.wait()
    h_hi, h_lo = hier_v[kind, 0], hier_v[kind, 1]
    there = [to_owners(0, advanced)]

    pass_edge()
    y, m, u = combinations(1)
    bent = basis @ interior @ left
    straight = float(basis[2] @ left)
    to_m = jnp.where(left_half[:1], 2.0 * straight * first_scale, 0.0)
    to_u = first_scale * jnp.where(
        left_half[:1],
        straight + 0.5 * float(bent[2]) * first_scale,
        0.5 * float(bent[3]) * first_scale,
    )
    to_u2 = jnp.where(left_half[:1], 0.5 * straight * first_scale, 0.0)
    edges = jnp.concatenate([edge_at(0, low) for low in range(LOW)], axis=0)
    plane[...] = u + to_u * edges + 0.5 * others_step(m + to_m * edges + others_step(y))
    second_edge.wait()
    edges = jnp.concatenate([edge_at(1, low) for low in range(LOW)], axis=0)
    there.append(to_owners(1, plane[...] + to_u2 * edges))

    coefs_copy.wait()

    def code_of(digits, comp):
        up2 = rise_of(comp, 1)
        up3 = rise_of(comp, 2)
        digit3 = digits & (lax.shift_left(one, up3) - 1)
        digit2 = lax.shift_right_logical(digits, jnp.full(digits.shape, up3)) & (
            lax.shift_left(one, up2) - 1
        )
        digit1 = lax.shift_right_logical(digits, jnp.full(digits.shape, up2 + up3))
        return digit1 * 64 + digit2 * 8 + digit3

    piece_row = lax.broadcasted_iota(jnp.int32, (8, 128), 0)
    piece_lane = lax.broadcasted_iota(jnp.int32, (8, 128), 1)
    lane_code = jnp.zeros((8, 128), jnp.int32)
    lane_coef = jnp.zeros((8, 128), F32)
    for comp in range(comps):
        own = lax.shift_right_logical(piece_lane, 3) == comp
        lane_code = jnp.where(own, code_of(piece_lane & 7, comp), lane_code)
        lane_coef = jnp.where(own, jnp.full((8, 128), coefs[comp].astype(F32)), lane_coef)
    for comp in range(0, comps, 2):
        block = [
            jnp.where(code_of(piece_row, here) == lane_code, lane_coef, 0.0)
            for here in (comp, comp + 1)
        ]
        match[8 * comp : 8 * comp + 16, :] = jnp.concatenate(block, axis=0).astype(BF16)

    cell_rows = lax.broadcasted_iota(jnp.int32, (GRID, 128), 0)
    lane_place = place_cell(piece_lane & (PLACES - 1))
    for part in range(GRID // 128):
        lane_cell = lane_place + jnp.where(
            piece_lane < 64, offsets[2 * part], offsets[2 * part + 1]
        )
        onehot[:, 128 * part : 128 * (part + 1)] = jnp.where(
            cell_rows == lane_cell[0:1, :], 1.0, 0.0
        ).astype(BF16)

    homeward = []
    for half in range(2):
        for copy in there[half]:
            copy.wait()
        for quarter in range(4):
            part = slice(8 * quarter, 8 * (quarter + 1))
            hi, lo = split(got[half, :, part, :].reshape(8 * comps, 128))
            both = dot(match[...], jnp.concatenate([hi, lo], axis=1))
            back[half, :, part, :] = fold(both).reshape(comps, 8, 128)
        homeward.append(exchange(back, home, half, back_send, back_recv, [(0, 2), (2, 8)] if half else ()))

    for half in range(2):
        for copy in homeward[half]:
            copy.wait()
        hi, lo = split(home[half].reshape(GRID, 128).T)
        both = dot(jnp.concatenate([hi, lo]), h_hi)
        plain = both[:128] + both[128:] + dot(hi, h_lo)
        for pair in range(LOW // 2):
            into = slice(128 * pair, 128 * (pair + 1))
            upper, lower = plain[:64, into], plain[64:, into]
            plane[block_of(2 * pair), :] = halves(upper, swap(lower))
            plane[block_of(2 * pair + 1), :] = halves(swap(upper), lower)
        pair = jnp.concatenate(split(plane[...]), axis=1)
        for part in range(4):
            cells = slice(128 * part, 128 * (part + 1))
            turned = fold(dot(onehot[cells, :], pair))
            swapped = swap(turned)
            for group in range(2):
                near = [float(basis[2 * half + k, 2 * group + k]) for k in range(2)]
                far = [float(basis[2 * half + 1 - k, 2 * group + k]) for k in range(2)]
                value = (
                    jnp.where(left_half[:1], near[0], near[1]) * turned
                    + jnp.where(left_half[:1], far[0], far[1]) * swapped
                )
                columns = slice(128 * group, 128 * (group + 1))
                if half == 0:
                    out_ref[0, 0, cells, columns] = value
                else:
                    out_ref[0, 0, cells, columns] += value


def on_device(modal_coefs, comp_levels, comp_coefs, velocity):
    comps = lax.axis_size("comp")
    shards = lax.axis_size("shard")
    stiff, lift, trace, hier = tables()
    anywhere = pl.BlockSpec(memory_space=pl.ANY)
    dma = pltpu.SemaphoreType.DMA
    exchanged = pltpu.VMEM((2, comps, GRID // comps, 128), F32)
    return pl.pallas_call(
        functools.partial(kernel, comps, shards),
        out_shape=pltpu.VMEM(modal_coefs.shape, F32),
        in_specs=[anywhere] * 8,
        out_specs=pl.BlockSpec(memory_space=pltpu.VMEM),
        scratch_shapes=[
            pltpu.SMEM((3, comps), jnp.int32),
            pltpu.SMEM((comps,), jnp.int32),
            pltpu.SMEM((4,), F32),
            pltpu.VMEM((GRID, COEF), F32),
            pltpu.VMEM(stiff.shape, F32),
            pltpu.VMEM(lift.shape, F32),
            pltpu.VMEM(trace.shape, BF16),
            pltpu.VMEM(hier.shape, BF16),
            pltpu.VMEM((GRID, GRID), BF16),
            pltpu.VMEM((8 * comps, 8 * comps), BF16),
            pltpu.VMEM((COEF, COEF), BF16),
            pltpu.VMEM((COEF, COEF), BF16),
            pltpu.VMEM((GRID, COEF), F32),
            pltpu.VMEM((GRID, COEF), F32),
            pltpu.VMEM((2 * LOW, PLACES, 128), F32),
            pltpu.VMEM((GRID, 128), F32),
            pltpu.VMEM((GRID, 128), F32),
            pltpu.VMEM((2, LOW // 2, PLACES, 128), F32),
            pltpu.VMEM((2, LOW // 2, PLACES, 128), F32),
            pltpu.VMEM((2, 2 * 128, GRID), BF16),
            exchanged,
            exchanged,
            exchanged,
            exchanged,
            dma((8,)),
            dma((2,)),
            dma((2,)),
            dma((2, comps)),
            dma((2, comps)),
            dma((2, comps)),
            dma((2, comps)),
        ],
        compiler_params=pltpu.CompilerParams(
            collective_id=0, has_side_effects=True, vmem_limit_bytes=VMEM_LIMIT
        ),
        name="combine",
    )(
        *[
            pltpu.with_memory_space_constraint(array, pltpu.HBM)
            for array in (
                comp_levels.T,
                comp_coefs,
                velocity,
                modal_coefs,
                jnp.asarray(stiff),
                jnp.asarray(lift),
                jnp.asarray(trace),
                jnp.asarray(hier),
            )
        ]
    )


def solution(mesh):
    placed = (P("comp", "shard", None, None), P(), P(), P())
    return jax.shard_map(
        on_device,
        mesh=mesh,
        in_specs=placed,
        out_specs=P("comp", "shard", None, None),
        check_vma=False,
    )
```

```python
import functools

import jax
import jax.numpy as jnp
import ml_dtypes
import numpy as np
from jax import lax
from jax.experimental import pallas as pl
from jax.experimental.pallas import tpu as pltpu
from jax.sharding import PartitionSpec as P

COEF = 256
BASE = 2
RISE = 3
GRID = 512
LOW = 2**RISE
PLACES = (2**BASE) ** 3
KINDS = (RISE + 1) * (RISE + 2) // 2
BF16 = jnp.bfloat16
F32 = jnp.float32
MESH = pl.DeviceIdType.MESH

courant = 0.1
VMEM_LIMIT = 48 * 2**20
ORDER = (4, 5, 3, 6, 2, 7, 1, 12, 13, 11, 14, 10, 15, 9, 8)
RIGHT_LEFT = float(sum((-1) ** order * (2 * order + 1) / 2.0 for order in range(4)))


def legendre(order, points):
    values = np.asarray(points) * 1.0
    if order == 0:
        poly = values * 0.0 + 1.0
    elif order == 1:
        poly = values
    elif order == 2:
        poly = (3.0 * values * values - 1.0) / 2.0
    else:
        poly = (5.0 * values * values * values - 3.0 * values) / 2.0
    return np.sqrt((2 * order + 1) / 2.0) * poly


def line_tables():
    nodes = np.array(
        [-0.8611363115940526, -0.3399810435848563, 0.3399810435848563, 0.8611363115940526]
    )
    weights = np.array(
        [0.3478548451374538, 0.6521451548625461, 0.6521451548625461, 0.3478548451374538]
    )
    stiff = np.zeros((4, 4))
    coarse = np.zeros((4, 8))
    for row in range(4):
        for column in range(4):
            if column < row and (row + column) % 2 == 1:
                stiff[row, column] = np.sqrt((2.0 * row + 1.0) * (2.0 * column + 1.0))
            coarse[row, column] = np.sum(
                weights * legendre(row, (nodes - 1.0) / 2.0) * legendre(column, nodes)
            ) / np.sqrt(2.0)
            coarse[row, column + 4] = np.sum(
                weights * legendre(row, (nodes + 1.0) / 2.0) * legendre(column, nodes)
            ) / np.sqrt(2.0)
    right = np.array([float(legendre(order, 1.0)) for order in range(4)])
    left = np.array([float(legendre(order, -1.0)) for order in range(4)])
    rows = [coarse[index] for index in range(4)]
    for index in range(4, 8):
        vector = np.eye(8)[index]
        for other in rows:
            vector = vector - np.dot(other, vector) * other
        rows.append(vector / np.sqrt(np.sum(vector * vector)))
    return (stiff - np.outer(right, right), right, left, np.array(rows))


def along(matrix, axis):
    return np.kron(np.eye(4**axis), np.kron(matrix, np.eye(4 ** (2 - axis))))


def twice(matrix):
    return np.kron(np.eye(2), matrix)


def first_basis():
    interior, _, left, _ = line_tables()
    turned, _ = np.linalg.qr(np.stack([left, interior @ left], axis=1), mode="complete")
    return np.concatenate([turned[:, 2:], turned[:, :2]], axis=1).T


def split_table(table):
    hi = table.astype(ml_dtypes.bfloat16)
    lo = (table - hi.astype(np.float64)).astype(ml_dtypes.bfloat16)
    return np.stack([hi, lo], axis=-3)


def line_hierarchy(filters, rise):
    cells = 2**rise
    whole = np.eye(cells * 4).reshape(cells, 4, cells * 4)
    for level_step in range(rise):
        for first in range(0, cells, 2 ** (level_step + 1)):
            second = first + 2**level_step
            pair = np.concatenate([whole[first], whole[second]], axis=0)
            mixed = filters @ pair
            whole[first], whole[second] = mixed[:4], mixed[4:]
    ordered = np.zeros_like(whole)
    for low in range(cells):
        digit = 0
        if low > 0:
            zeros = (low & -low).bit_length() - 1
            height = rise - zeros
            digit = 2 ** (height - 1) + (low >> (zeros + 1))
        ordered[digit] = whole[low]
    return ordered.reshape(cells, 4, cells, 4)


def compositions():
    return [(a, b, RISE - a - b) for a in range(RISE + 1) for b in range(RISE + 1 - a)]


@functools.lru_cache(None)
def tables():
    interior, right, left, filters = line_tables()
    stiff = np.stack([twice(along(interior, axis).T) for axis in range(3)]).astype(np.float32)
    lift = np.zeros((128, 128), np.float32)
    trace = np.zeros((128, 128))
    for axis in range(3):
        lift[32 * axis : 32 * (axis + 1)] = twice(along(left[:, None], axis).T)
        trace[:, 32 * axis : 32 * (axis + 1)] = twice(along(right[None, :], axis).T)
    lines = [line_hierarchy(filters, rise) for rise in range(RISE + 1)]
    hier = []
    for one, two, three in compositions():
        whole = np.einsum("aqlp,brms,cuno->qruabclmnpso", lines[one], lines[two], lines[three])
        hier.append(whole.reshape(GRID, GRID))
    hi, lo = split_table(trace)
    trace = np.block([[hi, lo], [hi, np.zeros_like(lo)]])
    return stiff, lift, trace, split_table(np.stack(hier))


def split(values):
    hi = values.astype(BF16)
    return hi, (values - hi.astype(F32)).astype(BF16)


def dot(one, two):
    return jnp.dot(one, two, preferred_element_type=F32)


def dot_nt(one, two):
    return lax.dot_general(one, two, (((1,), (1,)), ((), ())), preferred_element_type=F32)


def fold(values):
    return values[:, :128] + values[:, 128:]


def square(matrix):
    hi, lo = split(matrix)
    zero = jnp.zeros_like(lo)
    return jnp.concatenate(
        [jnp.concatenate([hi, lo], axis=1), jnp.concatenate([hi, zero], axis=1)], axis=0
    )


def kernel(
    comps,
    shards,
    levels_hbm,
    coefs_hbm,
    velocity_hbm,
    x_hbm,
    stiff_hbm,
    lift_hbm,
    trace_hbm,
    hier_hbm,
    out_ref,
    levels,
    coefs,
    velocity,
    x_v,
    stiff_v,
    lift_v,
    trace_v,
    hier_v,
    onehot,
    match,
    wide,
    lifts,
    field,
    other,
    traces,
    shifted,
    plane,
    edge_out,
    edge_in,
    rows,
    sent,
    got,
    back,
    home,
    local_sem,
    edge_send,
    edge_recv,
    there_send,
    there_recv,
    back_send,
    back_recv,
):
    me = lax.axis_index("comp")
    spot = lax.axis_index("shard")
    ahead = lax.rem(spot + 1, shards)
    behind = lax.rem(spot + shards - 1, shards)

    def fetch(source, target, index):
        copy = pltpu.make_async_copy(source, target, local_sem.at[index])
        copy.start()
        return copy

    levels_copy = fetch(levels_hbm, levels, 0)
    x_copy = fetch(x_hbm.at[0, 0], x_v, 1)
    velocity_copy = fetch(velocity_hbm, velocity, 2)
    trace_copy = fetch(trace_hbm, trace_v, 3)
    stiff_copy = fetch(stiff_hbm, stiff_v, 4)
    lift_copy = fetch(lift_hbm, lift_v, 5)
    coefs_copy = fetch(coefs_hbm, coefs, 6)
    hier_copy = fetch(hier_hbm, hier_v, 7)

    barrier = pltpu.get_barrier_semaphore()
    for step in range(1, comps):
        pl.semaphore_signal(
            barrier, inc=1, device_id={"comp": lax.rem(me + step, comps)}, device_id_type=MESH
        )
    pl.semaphore_signal(barrier, inc=1, device_id={"shard": behind}, device_id_type=MESH)

    levels_copy.wait()

    def rise_of(comp, axis):
        return jnp.clip(levels[axis, comp] - BASE, 0, RISE)

    rise1 = rise_of(me, 0)
    rise2 = rise_of(me, 1)
    rise3 = rise_of(me, 2)
    kind = jnp.clip(lax.shift_right_logical(rise1 * (9 - rise1), 1) + rise2, 0, KINDS - 1)
    one = jnp.int32(1)

    def low_digits(low):
        low3 = low & (lax.shift_left(one, rise3) - 1)
        low2 = lax.shift_right_logical(low, rise3) & (lax.shift_left(one, rise2) - 1)
        low1 = lax.shift_right_logical(low, rise2 + rise3)
        return low1, low2, low3

    def cell_of(digit1, digit2, digit3):
        return (
            lax.shift_left(digit1, rise2 + rise3 + 2 * BASE)
            + lax.shift_left(digit2, rise3 + BASE)
            + digit3
        )

    offsets = [cell_of(*low_digits(jnp.int32(low))) for low in range(LOW)]

    def place_cell(place):
        return cell_of(
            lax.shift_left(lax.shift_right_logical(place, 4) & 3, jnp.full(place.shape, rise1)),
            lax.shift_left(lax.shift_right_logical(place, 2) & 3, jnp.full(place.shape, rise2)),
            lax.shift_left(place & 3, jnp.full(place.shape, rise3)),
        )

    place_row = lax.broadcasted_iota(jnp.int32, (PLACES, 128), 0)
    lanes = lax.broadcasted_iota(jnp.int32, (PLACES, 128), 1)
    left_half = lanes < 64
    place_rows = place_cell(place_row)
    for low in range(LOW):
        for part in range(GRID // 128):
            hit = (place_rows + offsets[low]) == (lanes + 128 * part)
            onehot[low * PLACES : (low + 1) * PLACES, 128 * part : 128 * (part + 1)] = jnp.where(
                hit, 1.0, 0.0
            ).astype(BF16)

    def halves(one, two):
        return jnp.where(left_half, one, two)

    def swap(values):
        return pltpu.roll(values, 64, 1)

    def block_of(low):
        return slice(low * PLACES, (low + 1) * PLACES)

    def blocks(values):
        return [values[block_of(low), :] for low in range(LOW)]

    velocity_copy.wait()
    reach = None
    for comp in range(comps):
        total = velocity[0] * (1.0 * shards)
        for axis in range(3):
            size = lax.shift_left(one, levels[axis, comp]).astype(F32)
            total = total + velocity[axis + 1] * size
        reach = total if reach is None else jnp.maximum(reach, total)
    step_size = jnp.full((1, 128), courant, F32) / jnp.full((1, 128), reach, F32)
    sizes = [jnp.float32(shards)] + [
        lax.shift_left(one, levels[axis, me]).astype(F32) for axis in range(3)
    ]
    first_scale, *scales = [
        step_size * (2.0 * velocity[axis] * sizes[axis]) for axis in range(4)
    ]
    stiff_copy.wait()
    wide[...] = square(
        scales[0] * stiff_v[0] + scales[1] * stiff_v[1] + scales[2] * stiff_v[2]
    )
    lift_copy.wait()
    scale_rows = [jnp.broadcast_to(scale, (32, 128)) for scale in scales]
    lifts[...] = square(
        jnp.concatenate([*scale_rows, jnp.zeros((32, 128), F32)], axis=0) * lift_v[...]
    )

    x_copy.wait()
    hi, lo = split(x_v[...])
    now = dot(onehot[...], hi) + dot(onehot[...], lo)
    field[...] = now
    other[:, :128] = swap(now[:, :128])
    other[:, 128:] = swap(now[:, 128:])

    basis = first_basis()
    interior, right, left, _ = line_tables()

    def pair_of(rows_of):
        return [
            jnp.where(left_half[:1], float(rows_of[0][first]), float(rows_of[1][second]))
            for first, second in ((0, 1), (1, 0), (2, 3), (3, 2))
        ]

    def mix(factors):
        return (
            factors[0] * field[:, :128]
            + factors[1] * other[:, :128]
            + factors[2] * field[:, 128:]
            + factors[3] * other[:, 128:]
        )

    def edge_copy(stage):
        return pltpu.make_async_remote_copy(
            src_ref=edge_out.at[stage],
            dst_ref=edge_in.at[stage],
            send_sem=edge_send.at[stage],
            recv_sem=edge_recv.at[stage],
            device_id={"shard": ahead},
            device_id_type=MESH,
        )

    def pack(stage, values):
        parts = blocks(values)
        for low in range(LOW // 2):
            edge_out[stage, low] = halves(parts[low], parts[low + LOW // 2])

    pack(0, mix(pair_of([right, right])))
    pl.semaphore_wait(barrier, comps)
    first_edge, second_edge = edge_copy(0), edge_copy(1)
    first_edge.start()

    def behind_of(low, axis):
        digits = list(low_digits(jnp.int32(low)))
        rise = (rise1, rise2, rise3)[axis]
        first = digits[axis] == 0
        digits[axis] = (digits[axis] + lax.shift_left(one, rise) - 1) & (
            lax.shift_left(one, rise) - 1
        )
        spot = (
            lax.shift_left(digits[0], rise2 + rise3) + lax.shift_left(digits[1], rise3) + digits[2]
        )
        return (spot & (LOW - 1)) + jnp.where(first, LOW, 0)

    sources = [[behind_of(low, axis) for axis in range(3)] for low in range(LOW)]

    def by_axis(one, two, three):
        return jnp.where(lanes < 32, one, jnp.where(lanes < 64, two, three))

    def others_step(values):
        pair = jnp.concatenate(split(values), axis=1)
        for low, now in enumerate(blocks(fold(dot(pair, trace_v[...])))):
            traces[low] = now
            traces[LOW + low] = by_axis(
                pltpu.roll(now, 16, 0),
                jnp.where(
                    (place_row & 15) < 4, pltpu.roll(now, PLACES - 12, 0), pltpu.roll(now, 4, 0)
                ),
                jnp.where(
                    (place_row & 3) < 1, pltpu.roll(now, PLACES - 3, 0), pltpu.roll(now, 1, 0)
                ),
            )
        inner = dot(pair, wide[...])
        for low in range(LOW):
            shifted[block_of(low), :] = by_axis(*[traces[source] for source in sources[low]])
        return fold(inner + dot(jnp.concatenate(split(shifted[...]), axis=1), lifts[...]))

    def combinations(half):
        plain, once, square_of = [
            pair_of(matrix[2 * half : 2 * half + 2])
            for matrix in (basis, basis @ interior, basis @ interior @ interior)
        ]
        step = first_scale
        return (
            mix(plain),
            mix([2.0 * (p + step * o) for p, o in zip(plain, once)]),
            mix([p + step * (o + 0.5 * step * q) for p, o, q in zip(plain, once, square_of)]),
        )

    def edge_at(stage, low):
        edge = edge_in[stage, low % (LOW // 2)]
        turned = swap(edge)
        return halves(edge, turned) if low < LOW // 2 else halves(turned, edge)


    def exchange(source, target, half, send_sem, recv_sem, turns=()):
        copies = []
        for step in ORDER:
            other = lax.rem(me + step, comps)
            copy = pltpu.make_async_remote_copy(
                src_ref=source.at[half, other],
                dst_ref=target.at[half, me],
                send_sem=send_sem.at[half, step],
                recv_sem=recv_sem.at[half, step],
                device_id={"comp": other},
                device_id_type=MESH,
            )
            copies.append((copy, lax.rem(other, 8)))
        for first, last in turns or [(0, 8)]:
            for copy, height in copies:
                if turns:
                    pl.when((height >= first) & (height < last))(copy.start)
                else:
                    copy.start()
        target[half, me] = source[half, me]
        return [copy for copy, _ in copies]

    odd_height = lax.rem(me, 2) == 1

    def one_copy(half, other, slot):
        return pltpu.make_async_remote_copy(
            src_ref=sent.at[half, other],
            dst_ref=got.at[half, me],
            send_sem=there_send.at[half, slot],
            recv_sem=there_recv.at[half, slot],
            device_id={"comp": other},
            device_id_type=MESH,
        )

    def to_owners(half, advanced):
        parts = blocks(advanced)
        for pair in range(LOW // 2):
            even, odd = parts[2 * pair], parts[2 * pair + 1]
            into = slice(128 * pair, 128 * (pair + 1))
            hi, lo = split(jnp.concatenate([halves(even, swap(odd)), halves(swap(even), odd)]))
            rows[half, :128, into] = hi
            rows[half, 128:, into] = lo
        copies = []
        for side in range(2):
            wing = jnp.where((me < comps // 2) ^ odd_height, side, 1 - side) * (comps // 2)
            of_wing = pl.ds(pl.multiple_of(wing * (GRID // comps), GRID // 2), GRID // 2)
            both = dot_nt(hier_v[kind, 0, of_wing, :], rows[half])
            whole = fold(both) + dot_nt(hier_v[kind, 1, of_wing, :], rows[half, :128])
            sent[half, pl.ds(wing, comps // 2)] = whole.reshape(comps // 2, GRID // comps, 128)
            cross = jnp.where(odd_height, 1 - side, side)
            for step in (4, 5, 3, 6, 2, 7, 1):
                other = lax.rem(me + 8 * cross, comps) // 8 * 8 + lax.rem(me + step, 8)
                copies.append(one_copy(half, other, 8 * cross + step))
                copies[-1].start()
        copies.append(one_copy(half, lax.rem(me + 8, comps), 8))
        copies[-1].start()
        got[half, me] = sent[half, me]
        return copies

    def pass_edge():
        first_edge.wait()
        for low in range(LOW // 2):
            edge_out[1, low] += (first_scale * RIGHT_LEFT) * edge_in[0, low]
        second_edge.start()

    trace_copy.wait()
    y, m, u = combinations(0)
    advanced = u + 0.5 * others_step(m + others_step(y))
    hier_copy.wait()
    h_hi, h_lo = hier_v[kind, 0], hier_v[kind, 1]
    there = [to_owners(0, advanced)]

    pack(1, mix([first_scale * part for part in pair_of([right @ interior] * 2)]))
    pass_edge()
    y, m, u = combinations(1)
    bent = basis @ interior @ left
    straight = float(basis[2] @ left)
    to_m = jnp.where(left_half[:1], 2.0 * straight * first_scale, 0.0)
    to_u = first_scale * jnp.where(
        left_half[:1],
        straight + 0.5 * float(bent[2]) * first_scale,
        0.5 * float(bent[3]) * first_scale,
    )
    to_u2 = jnp.where(left_half[:1], 0.5 * straight * first_scale, 0.0)
    edges = jnp.concatenate([edge_at(0, low) for low in range(LOW)], axis=0)
    plane[...] = u + to_u * edges + 0.5 * others_step(m + to_m * edges + others_step(y))
    second_edge.wait()
    edges = jnp.concatenate([edge_at(1, low) for low in range(LOW)], axis=0)
    there.append(to_owners(1, plane[...] + to_u2 * edges))

    coefs_copy.wait()

    def code_of(digits, comp):
        up2 = rise_of(comp, 1)
        up3 = rise_of(comp, 2)
        digit3 = digits & (lax.shift_left(one, up3) - 1)
        digit2 = lax.shift_right_logical(digits, jnp.full(digits.shape, up3)) & (
            lax.shift_left(one, up2) - 1
        )
        digit1 = lax.shift_right_logical(digits, jnp.full(digits.shape, up2 + up3))
        return digit1 * 64 + digit2 * 8 + digit3

    piece_row = lax.broadcasted_iota(jnp.int32, (8, 128), 0)
    piece_lane = lax.broadcasted_iota(jnp.int32, (8, 128), 1)
    lane_code = jnp.zeros((8, 128), jnp.int32)
    lane_coef = jnp.zeros((8, 128), F32)
    for comp in range(comps):
        own = lax.shift_right_logical(piece_lane, 3) == comp
        lane_code = jnp.where(own, code_of(piece_lane & 7, comp), lane_code)
        lane_coef = jnp.where(own, jnp.full((8, 128), coefs[comp].astype(F32)), lane_coef)
    for comp in range(0, comps, 2):
        block = [
            jnp.where(code_of(piece_row, here) == lane_code, lane_coef, 0.0)
            for here in (comp, comp + 1)
        ]
        match[8 * comp : 8 * comp + 16, :] = jnp.concatenate(block, axis=0).astype(BF16)

    cell_rows = lax.broadcasted_iota(jnp.int32, (GRID, 128), 0)
    lane_place = place_cell(piece_lane & (PLACES - 1))
    for part in range(GRID // 128):
        lane_cell = lane_place + jnp.where(
            piece_lane < 64, offsets[2 * part], offsets[2 * part + 1]
        )
        onehot[:, 128 * part : 128 * (part + 1)] = jnp.where(
            cell_rows == lane_cell[0:1, :], 1.0, 0.0
        ).astype(BF16)

    homeward = []
    for half in range(2):
        for copy in there[half]:
            copy.wait()
        for quarter in range(4):
            part = slice(8 * quarter, 8 * (quarter + 1))
            hi, lo = split(got[half, :, part, :].reshape(8 * comps, 128))
            both = dot(match[...], jnp.concatenate([hi, lo], axis=1))
            back[half, :, part, :] = fold(both).reshape(comps, 8, 128)
        homeward.append(exchange(back, home, half, back_send, back_recv, [(0, 2), (2, 8)] if half else ()))

    for half in range(2):
        for copy in homeward[half]:
            copy.wait()
        hi, lo = split(home[half].reshape(GRID, 128).T)
        both = dot(jnp.concatenate([hi, lo]), h_hi)
        plain = both[:128] + both[128:] + dot(hi, h_lo)
        for pair in range(LOW // 2):
            into = slice(128 * pair, 128 * (pair + 1))
            upper, lower = plain[:64, into], plain[64:, into]
            plane[block_of(2 * pair), :] = halves(upper, swap(lower))
            plane[block_of(2 * pair + 1), :] = halves(swap(upper), lower)
        pair = jnp.concatenate(split(plane[...]), axis=1)
        for part in range(4):
            cells = slice(128 * part, 128 * (part + 1))
            turned = fold(dot(onehot[cells, :], pair))
            swapped = swap(turned)
            for group in range(2):
                near = [float(basis[2 * half + k, 2 * group + k]) for k in range(2)]
                far = [float(basis[2 * half + 1 - k, 2 * group + k]) for k in range(2)]
                value = (
                    jnp.where(left_half[:1], near[0], near[1]) * turned
                    + jnp.where(left_half[:1], far[0], far[1]) * swapped
                )
                columns = slice(128 * group, 128 * (group + 1))
                if half == 0:
                    out_ref[0, 0, cells, columns] = value
                else:
                    out_ref[0, 0, cells, columns] += value


def on_device(modal_coefs, comp_levels, comp_coefs, velocity):
    comps = lax.axis_size("comp")
    shards = lax.axis_size("shard")
    stiff, lift, trace, hier = tables()
    anywhere = pl.BlockSpec(memory_space=pl.ANY)
    dma = pltpu.SemaphoreType.DMA
    exchanged = pltpu.VMEM((2, comps, GRID // comps, 128), F32)
    return pl.pallas_call(
        functools.partial(kernel, comps, shards),
        out_shape=pltpu.VMEM(modal_coefs.shape, F32),
        in_specs=[anywhere] * 8,
        out_specs=pl.BlockSpec(memory_space=pltpu.VMEM),
        scratch_shapes=[
            pltpu.SMEM((3, comps), jnp.int32),
            pltpu.SMEM((comps,), jnp.int32),
            pltpu.SMEM((4,), F32),
            pltpu.VMEM((GRID, COEF), F32),
            pltpu.VMEM(stiff.shape, F32),
            pltpu.VMEM(lift.shape, F32),
            pltpu.VMEM(trace.shape, BF16),
            pltpu.VMEM(hier.shape, BF16),
            pltpu.VMEM((GRID, GRID), BF16),
            pltpu.VMEM((8 * comps, 8 * comps), BF16),
            pltpu.VMEM((COEF, COEF), BF16),
            pltpu.VMEM((COEF, COEF), BF16),
            pltpu.VMEM((GRID, COEF), F32),
            pltpu.VMEM((GRID, COEF), F32),
            pltpu.VMEM((2 * LOW, PLACES, 128), F32),
            pltpu.VMEM((GRID, 128), F32),
            pltpu.VMEM((GRID, 128), F32),
            pltpu.VMEM((2, LOW // 2, PLACES, 128), F32),
            pltpu.VMEM((2, LOW // 2, PLACES, 128), F32),
            pltpu.VMEM((2, 2 * 128, GRID), BF16),
            exchanged,
            exchanged,
            exchanged,
            exchanged,
            dma((8,)),
            dma((2,)),
            dma((2,)),
            dma((2, comps)),
            dma((2, comps)),
            dma((2, comps)),
            dma((2, comps)),
        ],
        compiler_params=pltpu.CompilerParams(
            collective_id=0, has_side_effects=True, vmem_limit_bytes=VMEM_LIMIT
        ),
        name="combine",
    )(
        *[
            pltpu.with_memory_space_constraint(array, pltpu.HBM)
            for array in (
                comp_levels.T,
                comp_coefs,
                velocity,
                modal_coefs,
                jnp.asarray(stiff),
                jnp.asarray(lift),
                jnp.asarray(trace),
                jnp.asarray(hier),
            )
        ]
    )


def solution(mesh):
    placed = (P("comp", "shard", None, None), P(), P(), P())
    return jax.shard_map(
        on_device,
        mesh=mesh,
        in_specs=placed,
        out_specs=P("comp", "shard", None, None),
        check_vma=False,
    )
```

```python
import functools

import jax
import jax.numpy as jnp
import ml_dtypes
import numpy as np
from jax import lax
from jax.experimental import pallas as pl
from jax.experimental.pallas import tpu as pltpu
from jax.sharding import PartitionSpec as P

COEF = 256
BASE = 2
RISE = 3
GRID = 512
LOW = 2**RISE
PLACES = (2**BASE) ** 3
KINDS = (RISE + 1) * (RISE + 2) // 2
BF16 = jnp.bfloat16
F32 = jnp.float32
MESH = pl.DeviceIdType.MESH

courant = 0.1
VMEM_LIMIT = 48 * 2**20
ORDER = (4, 5, 3, 6, 2, 7, 1, 12, 13, 11, 14, 10, 15, 9, 8)
RIGHT_LEFT = float(sum((-1) ** order * (2 * order + 1) / 2.0 for order in range(4)))


def legendre(order, points):
    values = np.asarray(points) * 1.0
    if order == 0:
        poly = values * 0.0 + 1.0
    elif order == 1:
        poly = values
    elif order == 2:
        poly = (3.0 * values * values - 1.0) / 2.0
    else:
        poly = (5.0 * values * values * values - 3.0 * values) / 2.0
    return np.sqrt((2 * order + 1) / 2.0) * poly


def line_tables():
    nodes = np.array(
        [-0.8611363115940526, -0.3399810435848563, 0.3399810435848563, 0.8611363115940526]
    )
    weights = np.array(
        [0.3478548451374538, 0.6521451548625461, 0.6521451548625461, 0.3478548451374538]
    )
    stiff = np.zeros((4, 4))
    coarse = np.zeros((4, 8))
    for row in range(4):
        for column in range(4):
            if column < row and (row + column) % 2 == 1:
                stiff[row, column] = np.sqrt((2.0 * row + 1.0) * (2.0 * column + 1.0))
            coarse[row, column] = np.sum(
                weights * legendre(row, (nodes - 1.0) / 2.0) * legendre(column, nodes)
            ) / np.sqrt(2.0)
            coarse[row, column + 4] = np.sum(
                weights * legendre(row, (nodes + 1.0) / 2.0) * legendre(column, nodes)
            ) / np.sqrt(2.0)
    right = np.array([float(legendre(order, 1.0)) for order in range(4)])
    left = np.array([float(legendre(order, -1.0)) for order in range(4)])
    rows = [coarse[index] for index in range(4)]
    for index in range(4, 8):
        vector = np.eye(8)[index]
        for other in rows:
            vector = vector - np.dot(other, vector) * other
        rows.append(vector / np.sqrt(np.sum(vector * vector)))
    return (stiff - np.outer(right, right), right, left, np.array(rows))


def along(matrix, axis):
    return np.kron(np.eye(4**axis), np.kron(matrix, np.eye(4 ** (2 - axis))))


def twice(matrix):
    return np.kron(np.eye(2), matrix)


def first_basis():
    interior, _, left, _ = line_tables()
    turned, _ = np.linalg.qr(np.stack([left, interior @ left], axis=1), mode="complete")
    return np.concatenate([turned[:, 2:], turned[:, :2]], axis=1).T


def split_table(table):
    hi = table.astype(ml_dtypes.bfloat16)
    lo = (table - hi.astype(np.float64)).astype(ml_dtypes.bfloat16)
    return np.stack([hi, lo], axis=-3)


def line_hierarchy(filters, rise):
    cells = 2**rise
    whole = np.eye(cells * 4).reshape(cells, 4, cells * 4)
    for level_step in range(rise):
        for first in range(0, cells, 2 ** (level_step + 1)):
            second = first + 2**level_step
            pair = np.concatenate([whole[first], whole[second]], axis=0)
            mixed = filters @ pair
            whole[first], whole[second] = mixed[:4], mixed[4:]
    ordered = np.zeros_like(whole)
    for low in range(cells):
        digit = 0
        if low > 0:
            zeros = (low & -low).bit_length() - 1
            height = rise - zeros
            digit = 2 ** (height - 1) + (low >> (zeros + 1))
        ordered[digit] = whole[low]
    return ordered.reshape(cells, 4, cells, 4)


def compositions():
    return [(a, b, RISE - a - b) for a in range(RISE + 1) for b in range(RISE + 1 - a)]


@functools.lru_cache(None)
def tables():
    interior, right, left, filters = line_tables()
    stiff = np.stack([twice(along(interior, axis).T) for axis in range(3)]).astype(np.float32)
    lift = np.zeros((128, 128), np.float32)
    trace = np.zeros((128, 128))
    for axis in range(3):
        lift[32 * axis : 32 * (axis + 1)] = twice(along(left[:, None], axis).T)
        trace[:, 32 * axis : 32 * (axis + 1)] = twice(along(right[None, :], axis).T)
    lines = [line_hierarchy(filters, rise) for rise in range(RISE + 1)]
    hier = []
    for one, two, three in compositions():
        whole = np.einsum("aqlp,brms,cuno->qruabclmnpso", lines[one], lines[two], lines[three])
        hier.append(whole.reshape(GRID, GRID))
    hi, lo = split_table(trace)
    trace = np.block([[hi, lo], [hi, np.zeros_like(lo)]])
    return stiff, lift, trace, split_table(np.stack(hier))


def split(values):
    hi = values.astype(BF16)
    return hi, (values - hi.astype(F32)).astype(BF16)


def dot(one, two):
    return jnp.dot(one, two, preferred_element_type=F32)


def dot_nt(one, two):
    return lax.dot_general(one, two, (((1,), (1,)), ((), ())), preferred_element_type=F32)


def fold(values):
    return values[:, :128] + values[:, 128:]


def square(matrix):
    hi, lo = split(matrix)
    zero = jnp.zeros_like(lo)
    return jnp.concatenate(
        [jnp.concatenate([hi, lo], axis=1), jnp.concatenate([hi, zero], axis=1)], axis=0
    )


def kernel(
    comps,
    shards,
    levels_hbm,
    coefs_hbm,
    velocity_hbm,
    x_hbm,
    stiff_hbm,
    lift_hbm,
    trace_hbm,
    hier_hbm,
    out_ref,
    levels,
    coefs,
    velocity,
    x_v,
    stiff_v,
    lift_v,
    trace_v,
    hier_v,
    onehot,
    match,
    wide,
    lifts,
    field,
    other,
    traces,
    shifted,
    plane,
    edge_out,
    edge_in,
    rows,
    sent,
    got,
    back,
    home,
    local_sem,
    edge_send,
    edge_recv,
    there_send,
    there_recv,
    back_send,
    back_recv,
):
    me = lax.axis_index("comp")
    spot = lax.axis_index("shard")
    ahead = lax.rem(spot + 1, shards)
    behind = lax.rem(spot + shards - 1, shards)

    def fetch(source, target, index):
        copy = pltpu.make_async_copy(source, target, local_sem.at[index])
        copy.start()
        return copy

    levels_copy = fetch(levels_hbm, levels, 0)
    x_copy = fetch(x_hbm.at[0, 0], x_v, 1)
    velocity_copy = fetch(velocity_hbm, velocity, 2)
    trace_copy = fetch(trace_hbm, trace_v, 3)
    stiff_copy = fetch(stiff_hbm, stiff_v, 4)
    lift_copy = fetch(lift_hbm, lift_v, 5)
    coefs_copy = fetch(coefs_hbm, coefs, 6)
    hier_copy = fetch(hier_hbm, hier_v, 7)

    barrier = pltpu.get_barrier_semaphore()
    for step in range(1, comps):
        pl.semaphore_signal(
            barrier, inc=1, device_id={"comp": lax.rem(me + step, comps)}, device_id_type=MESH
        )
    pl.semaphore_signal(barrier, inc=1, device_id={"shard": behind}, device_id_type=MESH)

    levels_copy.wait()

    def rise_of(comp, axis):
        return jnp.clip(levels[axis, comp] - BASE, 0, RISE)

    rise1 = rise_of(me, 0)
    rise2 = rise_of(me, 1)
    rise3 = rise_of(me, 2)
    kind = jnp.clip(lax.shift_right_logical(rise1 * (9 - rise1), 1) + rise2, 0, KINDS - 1)
    one = jnp.int32(1)

    def low_digits(low):
        low3 = low & (lax.shift_left(one, rise3) - 1)
        low2 = lax.shift_right_logical(low, rise3) & (lax.shift_left(one, rise2) - 1)
        low1 = lax.shift_right_logical(low, rise2 + rise3)
        return low1, low2, low3

    def cell_of(digit1, digit2, digit3):
        return (
            lax.shift_left(digit1, rise2 + rise3 + 2 * BASE)
            + lax.shift_left(digit2, rise3 + BASE)
            + digit3
        )

    offsets = [cell_of(*low_digits(jnp.int32(low))) for low in range(LOW)]

    def place_cell(place):
        return cell_of(
            lax.shift_left(lax.shift_right_logical(place, 4) & 3, jnp.full(place.shape, rise1)),
            lax.shift_left(lax.shift_right_logical(place, 2) & 3, jnp.full(place.shape, rise2)),
            lax.shift_left(place & 3, jnp.full(place.shape, rise3)),
        )

    place_row = lax.broadcasted_iota(jnp.int32, (PLACES, 128), 0)
    lanes = lax.broadcasted_iota(jnp.int32, (PLACES, 128), 1)
    left_half = lanes < 64
    place_rows = place_cell(place_row)
    for low in range(LOW):
        for part in range(GRID // 128):
            hit = (place_rows + offsets[low]) == (lanes + 128 * part)
            onehot[low * PLACES : (low + 1) * PLACES, 128 * part : 128 * (part + 1)] = jnp.where(
                hit, 1.0, 0.0
            ).astype(BF16)

    def halves(one, two):
        return jnp.where(left_half, one, two)

    def swap(values):
        return pltpu.roll(values, 64, 1)

    def block_of(low):
        return slice(low * PLACES, (low + 1) * PLACES)

    def blocks(values):
        return [values[block_of(low), :] for low in range(LOW)]

    velocity_copy.wait()
    reach = None
    for comp in range(comps):
        total = velocity[0] * (1.0 * shards)
        for axis in range(3):
            size = lax.shift_left(one, levels[axis, comp]).astype(F32)
            total = total + velocity[axis + 1] * size
        reach = total if reach is None else jnp.maximum(reach, total)
    step_size = jnp.full((1, 128), courant, F32) / jnp.full((1, 128), reach, F32)
    sizes = [jnp.float32(shards)] + [
        lax.shift_left(one, levels[axis, me]).astype(F32) for axis in range(3)
    ]
    first_scale, *scales = [
        step_size * (2.0 * velocity[axis] * sizes[axis]) for axis in range(4)
    ]
    stiff_copy.wait()
    wide[...] = square(
        scales[0] * stiff_v[0] + scales[1] * stiff_v[1] + scales[2] * stiff_v[2]
    )
    lift_copy.wait()
    scale_rows = [jnp.broadcast_to(scale, (32, 128)) for scale in scales]
    lifts[...] = square(
        jnp.concatenate([*scale_rows, jnp.zeros((32, 128), F32)], axis=0) * lift_v[...]
    )

    x_copy.wait()
    hi, lo = split(x_v[...])
    now = dot(onehot[...], hi) + dot(onehot[...], lo)
    field[...] = now
    other[:, :128] = swap(now[:, :128])
    other[:, 128:] = swap(now[:, 128:])

    basis = first_basis()
    interior, right, left, _ = line_tables()

    def pair_of(rows_of):
        return [
            jnp.where(left_half[:1], float(rows_of[0][first]), float(rows_of[1][second]))
            for first, second in ((0, 1), (1, 0), (2, 3), (3, 2))
        ]

    def mix(factors):
        return (
            factors[0] * field[:, :128]
            + factors[1] * other[:, :128]
            + factors[2] * field[:, 128:]
            + factors[3] * other[:, 128:]
        )

    def edge_copy(stage):
        return pltpu.make_async_remote_copy(
            src_ref=edge_out.at[stage],
            dst_ref=edge_in.at[stage],
            send_sem=edge_send.at[stage],
            recv_sem=edge_recv.at[stage],
            device_id={"shard": ahead},
            device_id_type=MESH,
        )

    def pack(stage, values):
        parts = blocks(values)
        for low in range(LOW // 2):
            edge_out[stage, low] = halves(parts[low], parts[low + LOW // 2])

    pack(0, mix(pair_of([right, right])))
    pl.semaphore_wait(barrier, comps)
    first_edge, second_edge = edge_copy(0), edge_copy(1)
    first_edge.start()

    def behind_of(low, axis):
        digits = list(low_digits(jnp.int32(low)))
        rise = (rise1, rise2, rise3)[axis]
        first = digits[axis] == 0
        digits[axis] = (digits[axis] + lax.shift_left(one, rise) - 1) & (
            lax.shift_left(one, rise) - 1
        )
        spot = (
            lax.shift_left(digits[0], rise2 + rise3) + lax.shift_left(digits[1], rise3) + digits[2]
        )
        return (spot & (LOW - 1)) + jnp.where(first, LOW, 0)

    sources = [[behind_of(low, axis) for axis in range(3)] for low in range(LOW)]

    def by_axis(one, two, three):
        return jnp.where(lanes < 32, one, jnp.where(lanes < 64, two, three))

    def others_step(values):
        pair = jnp.concatenate(split(values), axis=1)
        for low, now in enumerate(blocks(fold(dot(pair, trace_v[...])))):
            traces[low] = now
            traces[LOW + low] = by_axis(
                pltpu.roll(now, 16, 0),
                jnp.where(
                    (place_row & 15) < 4, pltpu.roll(now, PLACES - 12, 0), pltpu.roll(now, 4, 0)
                ),
                jnp.where(
                    (place_row & 3) < 1, pltpu.roll(now, PLACES - 3, 0), pltpu.roll(now, 1, 0)
                ),
            )
        inner = dot(pair, wide[...])
        for low in range(LOW):
            shifted[block_of(low), :] = by_axis(*[traces[source] for source in sources[low]])
        return fold(inner + dot(jnp.concatenate(split(shifted[...]), axis=1), lifts[...]))

    def combinations(half):
        plain, once, square_of = [
            pair_of(matrix[2 * half : 2 * half + 2])
            for matrix in (basis, basis @ interior, basis @ interior @ interior)
        ]
        step = first_scale
        return (
            mix(plain),
            mix([2.0 * (p + step * o) for p, o in zip(plain, once)]),
            mix([p + step * (o + 0.5 * step * q) for p, o, q in zip(plain, once, square_of)]),
        )

    def edge_at(stage, low):
        edge = edge_in[stage, low % (LOW // 2)]
        turned = swap(edge)
        return halves(edge, turned) if low < LOW // 2 else halves(turned, edge)


    def exchange(source, target, half, send_sem, recv_sem, turns=()):
        copies = []
        for step in ORDER:
            other = lax.rem(me + step, comps)
            copy = pltpu.make_async_remote_copy(
                src_ref=source.at[half, other],
                dst_ref=target.at[half, me],
                send_sem=send_sem.at[half, step],
                recv_sem=recv_sem.at[half, step],
                device_id={"comp": other},
                device_id_type=MESH,
            )
            copies.append((copy, lax.rem(other, 8)))
        for first, last in turns or [(0, 8)]:
            for copy, height in copies:
                if turns:
                    pl.when((height >= first) & (height < last))(copy.start)
                else:
                    copy.start()
        target[half, me] = source[half, me]
        return [copy for copy, _ in copies]

    odd_height = lax.rem(me, 2) == 1

    def one_copy(half, other, slot):
        return pltpu.make_async_remote_copy(
            src_ref=sent.at[half, other],
            dst_ref=got.at[half, me],
            send_sem=there_send.at[half, slot],
            recv_sem=there_recv.at[half, slot],
            device_id={"comp": other},
            device_id_type=MESH,
        )

    def to_owners(half, advanced):
        parts = blocks(advanced)
        for pair in range(LOW // 2):
            even, odd = parts[2 * pair], parts[2 * pair + 1]
            into = slice(128 * pair, 128 * (pair + 1))
            hi, lo = split(jnp.concatenate([halves(even, swap(odd)), halves(swap(even), odd)]))
            rows[half, :128, into] = hi
            rows[half, 128:, into] = lo
        copies = []
        for side in range(2):
            wing = jnp.where((me < comps // 2) ^ odd_height, side, 1 - side) * (comps // 2)
            of_wing = pl.ds(pl.multiple_of(wing * (GRID // comps), GRID // 2), GRID // 2)
            both = dot_nt(hier_v[kind, 0, of_wing, :], rows[half])
            whole = fold(both) + dot_nt(hier_v[kind, 1, of_wing, :], rows[half, :128])
            sent[half, pl.ds(wing, comps // 2)] = whole.reshape(comps // 2, GRID // comps, 128)
            cross = jnp.where(odd_height, 1 - side, side)
            for step in (4, 5, 3, 6, 2, 7, 1):
                other = lax.rem(me + 8 * cross, comps) // 8 * 8 + lax.rem(me + step, 8)
                copies.append(one_copy(half, other, 8 * cross + step))
                copies[-1].start()
        copies.append(one_copy(half, lax.rem(me + 8, comps), 8))
        copies[-1].start()
        got[half, me] = sent[half, me]
        return copies

    def pass_edge():
        first_edge.wait()
        for low in range(LOW // 2):
            edge_out[1, low] += (first_scale * RIGHT_LEFT) * edge_in[0, low]
        second_edge.start()

    trace_copy.wait()
    y, m, u = combinations(0)
    advanced = u + 0.5 * others_step(m + others_step(y))
    hier_copy.wait()
    h_hi, h_lo = hier_v[kind, 0], hier_v[kind, 1]
    there = [to_owners(0, advanced)]

    pack(1, mix([first_scale * part for part in pair_of([right @ interior] * 2)]))
    pl.when(lax.rem(spot, 2) == 1)(pass_edge)
    y, m, u = combinations(1)
    plane[...] = m + others_step(y)
    pl.when(lax.rem(spot, 2) == 0)(pass_edge)
    bent = basis @ interior @ left
    straight = float(basis[2] @ left)
    to_m = jnp.where(left_half[:1], 2.0 * straight * first_scale, 0.0)
    to_u = first_scale * jnp.where(
        left_half[:1],
        straight + 0.5 * float(bent[2]) * first_scale,
        0.5 * float(bent[3]) * first_scale,
    )
    to_u2 = jnp.where(left_half[:1], 0.5 * straight * first_scale, 0.0)
    edges = jnp.concatenate([edge_at(0, low) for low in range(LOW)], axis=0)
    plane[...] = u + to_u * edges + 0.5 * others_step(plane[...] + to_m * edges)
    second_edge.wait()
    edges = jnp.concatenate([edge_at(1, low) for low in range(LOW)], axis=0)
    there.append(to_owners(1, plane[...] + to_u2 * edges))

    coefs_copy.wait()

    def code_of(digits, comp):
        up2 = rise_of(comp, 1)
        up3 = rise_of(comp, 2)
        digit3 = digits & (lax.shift_left(one, up3) - 1)
        digit2 = lax.shift_right_logical(digits, jnp.full(digits.shape, up3)) & (
            lax.shift_left(one, up2) - 1
        )
        digit1 = lax.shift_right_logical(digits, jnp.full(digits.shape, up2 + up3))
        return digit1 * 64 + digit2 * 8 + digit3

    piece_row = lax.broadcasted_iota(jnp.int32, (8, 128), 0)
    piece_lane = lax.broadcasted_iota(jnp.int32, (8, 128), 1)
    lane_code = jnp.zeros((8, 128), jnp.int32)
    lane_coef = jnp.zeros((8, 128), F32)
    for comp in range(comps):
        own = lax.shift_right_logical(piece_lane, 3) == comp
        lane_code = jnp.where(own, code_of(piece_lane & 7, comp), lane_code)
        lane_coef = jnp.where(own, jnp.full((8, 128), coefs[comp].astype(F32)), lane_coef)
    for comp in range(0, comps, 2):
        block = [
            jnp.where(code_of(piece_row, here) == lane_code, lane_coef, 0.0)
            for here in (comp, comp + 1)
        ]
        match[8 * comp : 8 * comp + 16, :] = jnp.concatenate(block, axis=0).astype(BF16)

    cell_rows = lax.broadcasted_iota(jnp.int32, (GRID, 128), 0)
    lane_place = place_cell(piece_lane & (PLACES - 1))
    for part in range(GRID // 128):
        lane_cell = lane_place + jnp.where(
            piece_lane < 64, offsets[2 * part], offsets[2 * part + 1]
        )
        onehot[:, 128 * part : 128 * (part + 1)] = jnp.where(
            cell_rows == lane_cell[0:1, :], 1.0, 0.0
        ).astype(BF16)

    homeward = []
    for half in range(2):
        for copy in there[half]:
            copy.wait()
        for quarter in range(4):
            part = slice(8 * quarter, 8 * (quarter + 1))
            hi, lo = split(got[half, :, part, :].reshape(8 * comps, 128))
            both = dot(match[...], jnp.concatenate([hi, lo], axis=1))
            back[half, :, part, :] = fold(both).reshape(comps, 8, 128)
        homeward.append(exchange(back, home, half, back_send, back_recv, [(0, 2), (2, 8)] if half else ()))

    for half in range(2):
        for copy in homeward[half]:
            copy.wait()
        hi, lo = split(home[half].reshape(GRID, 128).T)
        both = dot(jnp.concatenate([hi, lo]), h_hi)
        plain = both[:128] + both[128:] + dot(hi, h_lo)
        for pair in range(LOW // 2):
            into = slice(128 * pair, 128 * (pair + 1))
            upper, lower = plain[:64, into], plain[64:, into]
            plane[block_of(2 * pair), :] = halves(upper, swap(lower))
            plane[block_of(2 * pair + 1), :] = halves(swap(upper), lower)
        pair = jnp.concatenate(split(plane[...]), axis=1)
        for part in range(4):
            cells = slice(128 * part, 128 * (part + 1))
            turned = fold(dot(onehot[cells, :], pair))
            swapped = swap(turned)
            for group in range(2):
                near = [float(basis[2 * half + k, 2 * group + k]) for k in range(2)]
                far = [float(basis[2 * half + 1 - k, 2 * group + k]) for k in range(2)]
                value = (
                    jnp.where(left_half[:1], near[0], near[1]) * turned
                    + jnp.where(left_half[:1], far[0], far[1]) * swapped
                )
                columns = slice(128 * group, 128 * (group + 1))
                if half == 0:
                    out_ref[0, 0, cells, columns] = value
                else:
                    out_ref[0, 0, cells, columns] += value


def on_device(modal_coefs, comp_levels, comp_coefs, velocity):
    comps = lax.axis_size("comp")
    shards = lax.axis_size("shard")
    stiff, lift, trace, hier = tables()
    anywhere = pl.BlockSpec(memory_space=pl.ANY)
    dma = pltpu.SemaphoreType.DMA
    exchanged = pltpu.VMEM((2, comps, GRID // comps, 128), F32)
    return pl.pallas_call(
        functools.partial(kernel, comps, shards),
        out_shape=pltpu.VMEM(modal_coefs.shape, F32),
        in_specs=[anywhere] * 8,
        out_specs=pl.BlockSpec(memory_space=pltpu.VMEM),
        scratch_shapes=[
            pltpu.SMEM((3, comps), jnp.int32),
            pltpu.SMEM((comps,), jnp.int32),
            pltpu.SMEM((4,), F32),
            pltpu.VMEM((GRID, COEF), F32),
            pltpu.VMEM(stiff.shape, F32),
            pltpu.VMEM(lift.shape, F32),
            pltpu.VMEM(trace.shape, BF16),
            pltpu.VMEM(hier.shape, BF16),
            pltpu.VMEM((GRID, GRID), BF16),
            pltpu.VMEM((8 * comps, 8 * comps), BF16),
            pltpu.VMEM((COEF, COEF), BF16),
            pltpu.VMEM((COEF, COEF), BF16),
            pltpu.VMEM((GRID, COEF), F32),
            pltpu.VMEM((GRID, COEF), F32),
            pltpu.VMEM((2 * LOW, PLACES, 128), F32),
            pltpu.VMEM((GRID, 128), F32),
            pltpu.VMEM((GRID, 128), F32),
            pltpu.VMEM((2, LOW // 2, PLACES, 128), F32),
            pltpu.VMEM((2, LOW // 2, PLACES, 128), F32),
            pltpu.VMEM((2, 2 * 128, GRID), BF16),
            exchanged,
            exchanged,
            exchanged,
            exchanged,
            dma((8,)),
            dma((2,)),
            dma((2,)),
            dma((2, comps)),
            dma((2, comps)),
            dma((2, comps)),
            dma((2, comps)),
        ],
        compiler_params=pltpu.CompilerParams(
            collective_id=0, has_side_effects=True, vmem_limit_bytes=VMEM_LIMIT
        ),
        name="combine",
    )(
        *[
            pltpu.with_memory_space_constraint(array, pltpu.HBM)
            for array in (
                comp_levels.T,
                comp_coefs,
                velocity,
                modal_coefs,
                jnp.asarray(stiff),
                jnp.asarray(lift),
                jnp.asarray(trace),
                jnp.asarray(hier),
            )
        ]
    )


def solution(mesh):
    placed = (P("comp", "shard", None, None), P(), P(), P())
    return jax.shard_map(
        on_device,
        mesh=mesh,
        in_specs=placed,
        out_specs=P("comp", "shard", None, None),
        check_vma=False,
    )
```
